128 devices in a mesh: cube: 16 (over y_lo, x, core), row: 4 (over z), col: 2 (over y_hi).
Axes of the slice: x: 4, y: 4 (y_hi: 2, y_lo: 2; y = y_hi * 2 + y_lo), z: 4, core: 2. Of those that a mesh axis runs over, the one named last changes fastest.
Arguments:
- update_tiles: float32 [16, 4, 2, 128, 128, 128], P('cube', 'row', 'col'), may hold values from -1.5 to 1.5
- split_order: int32 [16, 4, 2, 4, 128], P('cube', 'row', 'col'), may hold values from 0 to 127, each once within a row
- first_source: int32 [16, 4, 2, 4, 128], P('cube', 'row', 'col'), may hold values from 0 to 127, each once within a row
- second_source: int32 [16, 4, 2, 4, 128], P('cube', 'row', 'col'), may hold values from 0 to 127
- pivot_inverse: float32 [512, 512], replicated, may hold values from -0.01171875 to 0.01171875
Outputs:
- schur: float32 [16, 4, 2, 512, 4096], P('cube', 'row', 'col')
The draws below stay inside these ranges and needn't reach their ends.
Inputs may be any that keep to these rules, and one draw needn't show every extreme that they name: Each level's list of split_order on a device holds every tile number once. Each level's list of first_source on a device holds every joined tile number once.
All inputs are finite; a program needn't handle non-finite values.
Results may differ from the reference program's by a relative error of at most 0.00013.
Values sent between devices are 32-bit elements; how exact they have to be, the bound alone decides.
No kernel may reach another device: no remote copies, remote signals or barrier semaphores. Data moves between devices by JAX's collectives and lax.ppermute only.
A program may use at most 128 MiB of HBM per device.

```python
import jax
import jax.numpy as jnp
from jax import lax

TB = 128
KR = 4
KC = 32
PW = 512
LEVELS = 4
K = 128
N_CUBE = 16
N_ROW = 4
N_COL = 2


def set_ends(entries, key, low, top_value):
    place = [jax.random.randint(jax.random.fold_in(key, axis), (), 0, length) for axis, length in enumerate(entries.shape)]
    widest = entries.shape.index(max(entries.shape))
    neighbour = place[:widest] + [(place[widest] + 1) % entries.shape[widest]] + place[widest + 1:]
    return entries.at[tuple(place)].set(low).at[tuple(neighbour)].set(top_value)


def block_scale(own_key, extent, split, low, high):
    def one(axis_at, blocks):
        draws = jax.random.uniform(jax.random.fold_in(jax.random.fold_in(own_key, 6), axis_at), (blocks,), jnp.float32, low / len(split), high / len(split))
        return jnp.repeat(jnp.exp(draws), extent[axis_at] // blocks).reshape((-1,) + (1,) * (len(extent) - axis_at - 1))

    gain = one(*split[0])
    for cut in split[1:]:
        gain = gain * one(*cut)
    return gain


def noise(rng, dims, deviation, bound, cuts=(), held_as=jnp.bfloat16):
    gain = block_scale(rng, dims, cuts, -0.22, 0.18) if cuts else 1.0
    array = jax.random.normal(rng, dims, jnp.float32) * deviation * gain
    return jnp.minimum(jnp.maximum(array, -bound), bound).astype(held_as)


def setup_inputs(seed: int = 0) -> dict:
    arg_keys = jax.random.split(jax.random.key(seed), 6)
    update_tiles = noise(arg_keys[0], (N_CUBE, N_ROW, N_COL, K, TB, TB), 0.25, 1.5, ((0, 16), (1, 4), (2, 2)), jnp.float32)
    split_order = jax.vmap(lambda own: jax.random.permutation(own, K))(jax.random.split(arg_keys[1], N_CUBE * N_ROW * N_COL * LEVELS)).reshape((N_CUBE, N_ROW, N_COL, LEVELS, K)).astype(jnp.int32)
    first_source = jax.vmap(lambda own: jax.random.permutation(own, K))(jax.random.split(arg_keys[2], N_CUBE * N_ROW * N_COL * LEVELS)).reshape((N_CUBE, N_ROW, N_COL, LEVELS, K)).astype(jnp.int32)
    second_source = set_ends(jax.random.randint(arg_keys[3], (N_CUBE, N_ROW, N_COL, LEVELS, K), 0, K), jax.random.fold_in(arg_keys[3], 1), 0, K - 1).astype(jnp.int32)
    pivot_inverse = noise(arg_keys[4], (PW, PW), (PW * PW) ** -0.5, 0.01171875, (), jnp.float32)
    return {"update_tiles": update_tiles, "split_order": split_order, "first_source": first_source, "second_source": second_source, "pivot_inverse": pivot_inverse}


def reference(update_tiles, split_order, first_source, second_source, pivot_inverse):
    front_tiles = update_tiles
    bit_count = N_CUBE.bit_length() - 1
    half_count = K // 2
    for level_index in range(LEVELS):
        swap_bit = level_index % bit_count
        stride = 2 ** swap_bit
        sent_order = split_order[:, :, :, level_index, :][..., None, None]
        arranged = jnp.take_along_axis(front_tiles, sent_order, axis=3)
        sent_tiles = arranged[:, :, :, :half_count]
        kept_tiles = arranged[:, :, :, half_count:]
        shaped = sent_tiles.reshape((N_CUBE // (2 * stride), 2, stride) + sent_tiles.shape[1:])
        received = shaped[:, ::-1].reshape(sent_tiles.shape)
        joined = jnp.concatenate([kept_tiles, received], axis=3)
        first_index = first_source[:, :, :, level_index, :][..., None, None]
        second_index = second_source[:, :, :, level_index, :][..., None, None]
        front_tiles = jnp.take_along_axis(joined, first_index, axis=3) + jnp.take_along_axis(joined, second_index, axis=3)
    grid = front_tiles.reshape(N_CUBE, N_ROW, N_COL, KR, KC, TB, TB)
    front_block = grid.transpose(0, 1, 2, 3, 5, 4, 6).reshape(N_CUBE, N_ROW, N_COL, KR * TB, KC * TB)
    pivot_cols = front_block[:, :, 0, :, :PW]
    pivot_rows = front_block[0, 0, :, :PW, :]
    panel_left = jnp.einsum("abrp,ps->abrs", pivot_cols, pivot_inverse, precision=lax.Precision.HIGHEST)
    update = jnp.einsum("abrs,qsc->abqrc", panel_left, pivot_rows, precision=lax.Precision.HIGHEST)
    return front_block - update
```

```python
import jax
import jax.numpy as jnp
from jax import lax
from jax.experimental import pallas as pl
from jax.experimental.pallas import tpu as pltpu
from jax.sharding import PartitionSpec as P

TB = 128
KR = 4
KC = 32
PW = 512
K = 128
HALF = 64
LEVELS = 4
F32 = jnp.float32
BF16 = jnp.bfloat16

CHUNKS = ((96, 16), (0, 32), (32, 32), (64, 32), (112, 16))
PARTS = ((0, 64), (64, 64))

ANY = pl.BlockSpec(memory_space=pl.ANY)
SMEM = pl.BlockSpec(memory_space=pltpu.SMEM)
VMEM = pl.BlockSpec(memory_space=pltpu.VMEM)
DMA = pltpu.SemaphoreType.DMA


def nt(a, b):
    return lax.dot_general(a, b, (((1,), (1,)), ((), ())), preferred_element_type=F32)


def split2(x):
    high = x.astype(BF16)
    return high, (x - high.astype(F32)).astype(BF16)


def run(body, ins, outs, scratch, limit=32, **more):
    return pl.pallas_call(
        body,
        in_specs=[s for _, s in ins],
        out_specs=[s for _, _, s in outs],
        out_shape=[jax.ShapeDtypeStruct(s, d) for s, d, _ in outs],
        scratch_shapes=scratch,
        compiler_params=pltpu.CompilerParams(vmem_limit_bytes=limit << 20),
        **more,
    )(*[a for a, _ in ins])


def first_send(row, rows, tiles, split, tok):
    def body(split_ref, tiles_ref, _, send_ref, pool, buf, sem):
        get = pltpu.make_async_copy(tiles_ref.at[:, pl.ds(row, rows), :], pool, sem.at[0])
        get.start()
        get.wait()

        def step(i, c):
            buf[i] = pool[split_ref[0, i]]
            return c

        lax.fori_loop(0, HALF, step, 0, unroll=8)
        put = pltpu.make_async_copy(buf, send_ref, sem.at[1])
        put.start()
        put.wait()

    return run(
        body,
        [(split, SMEM), (tiles, ANY), (tok, ANY)],
        [((HALF, rows, TB), F32, ANY)],
        [pltpu.VMEM((K, rows, TB), F32), pltpu.VMEM((HALF, rows, TB), F32), DMA((2,))],
    )


def fetch(level, row, rows, kept_ref, recv_ref, pool, sem):
    own = kept_ref.at[:, pl.ds(row, rows), :] if level == 0 else kept_ref
    n = K if level == 0 else HALF
    one = pltpu.make_async_copy(own, pool.at[pl.ds(0, n)], sem.at[0])
    two = pltpu.make_async_copy(recv_ref, pool.at[pl.ds(n, HALF)], sem.at[1])
    one.start()
    two.start()
    one.wait()
    two.wait()


def place(level, split_ref, j):
    if level == 0:
        return jnp.where(j < HALF, split_ref[0, (j + HALF) & (K - 1)], j + HALF)
    return j


def next_level(level, row, rows, kept, recv, split, first, second, tok):
    n = K if level == 0 else HALF

    def body(split_ref, first_ref, second_ref, kept_ref, recv_ref, _, send_ref, keep_ref, pool, buf, sem):
        fetch(level, row, rows, kept_ref, recv_ref, pool, sem)

        def step(i, c):
            t = split_ref[level + 1, i]
            a = place(level, split_ref, first_ref[level, t])
            b = place(level, split_ref, second_ref[level, t])
            buf[i] = pool[a] + pool[b]
            return c

        lax.fori_loop(0, HALF, step, 0, unroll=8)
        one = pltpu.make_async_copy(buf.at[pl.ds(0, HALF)], send_ref, sem.at[2])
        one.start()
        lax.fori_loop(HALF, K, step, 0, unroll=8)
        two = pltpu.make_async_copy(buf.at[pl.ds(HALF, HALF)], keep_ref, sem.at[3])
        two.start()
        one.wait()
        two.wait()

    return run(
        body,
        [(split, SMEM), (first, SMEM), (second, SMEM), (kept, ANY), (recv, ANY), (tok, ANY)],
        [((HALF, rows, TB), F32, ANY)] * 2,
        [pltpu.VMEM((n + HALF, rows, TB), F32), pltpu.VMEM((K, rows, TB), F32), DMA((4,))],
    )


def last_level(rows, kept, recv, first, second, tok):
    def body(first_ref, second_ref, kept_ref, recv_ref, _, cols_ref, front_ref, pool, buf, cbuf, sem):
        level = LEVELS - 1
        fetch(level, 0, rows, kept_ref, recv_ref, pool, sem)
        for i in range(KR):
            for j in range(PW // TB):
                t = i * KC + j
                tile = pool[first_ref[level, t]] + pool[second_ref[level, t]]
                buf[i, :, j * TB:(j + 1) * TB] = tile
                cbuf[i, :, j * TB:(j + 1) * TB] = tile
        one = pltpu.make_async_copy(cbuf, cols_ref, sem.at[2])
        one.start()
        for i in range(KR):

            def step(j, c):
                t = i * KC + j
                at = pl.ds(pl.multiple_of(j * TB, TB), TB)
                buf[i, :, at] = pool[first_ref[level, t]] + pool[second_ref[level, t]]
                return c

            lax.fori_loop(PW // TB, KC, step, 0, unroll=4)
        two = pltpu.make_async_copy(buf, front_ref, sem.at[3])
        two.start()
        one.wait()
        two.wait()

    return run(
        body,
        [(first, SMEM), (second, SMEM), (kept, ANY), (recv, ANY), (tok, ANY)],
        [((KR, rows, PW), F32, ANY), ((KR, rows, KC * TB), F32, ANY)],
        [
            pltpu.VMEM((K, rows, TB), F32),
            pltpu.VMEM((KR, rows, KC * TB), F32),
            pltpu.VMEM((KR, rows, PW), F32),
            DMA((4,)),
        ],
    )


def joined_weights(own, other):
    lane = lax.broadcasted_iota(jnp.int32, (K, K), 1)
    return jnp.where(lane < HALF, own, other)


def weights_back(level, own, other, place_ids, lists, tok):
    top = level == LEVELS - 1

    def body(ids_ref, lists_ref, *refs):
        out_ref = refs[-1]
        row = lax.broadcasted_iota(jnp.int32, (K, K), 0)
        lane = lax.broadcasted_iota(jnp.int32, (K, K), 1)
        if top:
            root = jnp.logical_and(ids_ref[0] == 0, ids_ref[1] == 0)
            weight = jnp.where(jnp.logical_and(row == lane, root), 1.0, 0.0)
        else:
            order = lists_ref[12 + level + 1: 13 + level + 1, :]
            joined = joined_weights(refs[0][...], refs[1][...])
            weight = nt(joined.astype(BF16), jnp.where(row == order, 1.0, 0.0).astype(BF16))
        one = jnp.where(row == lists_ref[4 + level: 5 + level, :], 1.0, 0.0)
        two = jnp.where(row == lists_ref[8 + level: 9 + level, :], 1.0, 0.0)
        out_ref[...] = jnp.dot(weight.astype(BF16), (one + two).T.astype(BF16), preferred_element_type=F32)

    ins = [(place_ids, SMEM), (lists, VMEM)]
    if not top:
        ins += [(own, VMEM), (other, VMEM)]
    return run(body, ins + [(tok, ANY)], [((K, K), F32, VMEM)], [])


def parts_of(row, rows, own, other, place_ids, lists, tiles, tok):
    def body(ids_ref, lists_ref, own_ref, other_ref, tiles_ref, _, keep_ref, send_ref, pool, buf, sem):
        get = pltpu.make_async_copy(tiles_ref.at[:, pl.ds(row, rows), :], pool, sem.at[0])
        get.start()
        r = lax.broadcasted_iota(jnp.int32, (K, K), 0)
        c = lax.broadcasted_iota(jnp.int32, (K, K), 1)
        joined = joined_weights(own_ref[...], other_ref[...]).astype(BF16)
        weight = nt(joined, jnp.where(r == lists_ref[12:13, :], 1.0, 0.0).astype(BF16)).astype(BF16)
        turn = jnp.where(c == jnp.bitwise_xor(r, ids_ref[3]), 1.0, 0.0).astype(BF16)
        weight = jnp.dot(turn, weight, preferred_element_type=F32).astype(BF16)
        get.wait()
        flat = pool.reshape(K * rows, TB)
        out = buf.reshape(K * rows, TB)

        def step(at, carry):
            high, low = split2(flat[pl.ds(at, K, stride=rows), :])
            out[pl.ds(at, K, stride=rows), :] = jnp.dot(weight, high, preferred_element_type=F32) + jnp.dot(
                weight, low, preferred_element_type=F32
            )
            return carry

        lax.fori_loop(0, rows, step, 0, unroll=4)
        one = pltpu.make_async_copy(buf.at[pl.ds(0, HALF)], keep_ref, sem.at[1])
        two = pltpu.make_async_copy(buf.at[pl.ds(HALF, HALF)], send_ref, sem.at[2])
        one.start()
        two.start()
        one.wait()
        two.wait()

    return run(
        body,
        [(place_ids, SMEM), (lists, VMEM), (own, VMEM), (other, VMEM), (tiles, ANY), (tok, ANY)],
        [((HALF, rows, TB), F32, ANY)] * 2,
        [pltpu.VMEM((K, rows, TB), F32), pltpu.VMEM((K, rows, TB), F32), DMA((3,))],
    )


def add_cut(terms, cuts, rows, tok):
    def body(*refs):
        total = refs[0][...]
        for term in refs[1:len(terms)]:
            total = total + term[...]
        at = 0
        for cut, ref in zip(cuts, refs[len(terms) + 1:]):
            ref[...] = total[at:at + cut]
            at += cut

    return run(
        body, [(t, VMEM) for t in terms] + [(tok, ANY)], [((cut, rows, TB), F32, VMEM) for cut in cuts], []
    )


def lay(pieces, rows, tok):
    count = sum(p.shape[0] for p in pieces)

    def body(*refs):
        out_ref, sem = refs[-2:]
        copies = []
        at = 0
        for n, piece in enumerate(pieces):
            copies.append(
                pltpu.make_async_copy(refs[n], out_ref.at[pl.ds(at, piece.shape[0])], sem.at[n])
            )
            at += piece.shape[0]
        for copy in copies:
            copy.start()
        for copy in copies:
            copy.wait()

    return run(body, [(p, ANY) for p in pieces] + [(tok, ANY)], [((count, rows, TB), F32, ANY)], [DMA((len(pieces),))])


def panel(row, rows, low, high, place_ids, inverse, before, last, tok):
    wide = 4
    width = wide * TB

    def body(*refs):
        ids_ref, inv_ref, low_ref, high_ref = refs[:4]
        before_ref = refs[4] if before is not None else None
        at = 5 if before is not None else 4
        outs = refs[at + 1: at + (3 if last else 2)]
        pool, rhs_h, rhs_l, sem = refs[-4:]
        one = pltpu.make_async_copy(low_ref, pool.at[pl.ds(0, HALF)], sem.at[0])
        two = pltpu.make_async_copy(high_ref, pool.at[pl.ds(HALF, HALF)], sem.at[1])
        one.start()
        two.start()
        mask = ids_ref[3]
        pieces = [split2(inv_ref[:, i * TB + row: i * TB + row + rows]) for i in range(KR)]
        inv_h = jnp.concatenate([p[0] for p in pieces], axis=1)
        inv_l = jnp.concatenate([p[1] for p in pieces], axis=1)
        one.wait()
        two.wait()

        def step(n, c):
            for j in range(wide):
                for i in range(KR):
                    s = jnp.bitwise_xor(i * KC + n * wide + j, mask)
                    slot = (s & 64) + ((s >> 3) & 3) * 16 + ((s >> 5) & 1) * 8 + (s & 7)
                    h, lo = split2(pool[slot])
                    rhs_h[i * rows:(i + 1) * rows, j * TB:(j + 1) * TB] = h
                    rhs_l[i * rows:(i + 1) * rows, j * TB:(j + 1) * TB] = lo
            h = rhs_h[...]
            total = jnp.dot(inv_h, h, preferred_element_type=F32)
            total += jnp.dot(inv_l, h, preferred_element_type=F32)
            total += jnp.dot(inv_h, rhs_l[...], preferred_element_type=F32)
            cols = pl.ds(pl.multiple_of(n * width, width), width)
            if before is not None:
                total += before_ref[:, cols]
            if last:
                outs[0][:, cols], outs[1][:, cols] = split2(total)
            else:
                outs[0][:, cols] = total
            return c

        lax.fori_loop(0, KC // wide, step, 0)

    ins = [(place_ids, SMEM), (inverse, VMEM), (low, ANY), (high, ANY)]
    if before is not None:
        ins.append((before, VMEM))
    shape = (PW, KC * TB)
    return run(
        body,
        ins + [(tok, ANY)],
        [(shape, BF16, VMEM)] * 2 if last else [(shape, F32, VMEM)],
        [
            pltpu.VMEM((K, rows, TB), F32),
            pltpu.VMEM((KR * rows, width), BF16),
            pltpu.VMEM((KR * rows, width), BF16),
            DMA((2,)),
        ],
        limit=48,
    )


def update(row, rows, front, cols, cols_sent, place_ids, high, low, out, tok):
    width = 1024

    def body(ids_ref, cols_ref, sent_ref, front_ref, high_ref, low_ref, *rest):
        out_ref = rest[-1]
        own = jnp.where(ids_ref[2] == 0, cols_ref[...], sent_ref[...]).reshape(KR * rows, PW)
        h, lo = split2(own)
        q = high_ref[...]
        total = jnp.dot(h, q, preferred_element_type=F32)
        total += jnp.dot(lo, q, preferred_element_type=F32)
        total += jnp.dot(h, low_ref[...], preferred_element_type=F32)
        out_ref[...] = front_ref[...] - total.reshape(KR, rows, width)

    pivot = pl.BlockSpec((KR, rows, PW), lambda n: (0, 0, 0))
    ins = [
        (place_ids, SMEM),
        (cols, pivot),
        (cols_sent, pivot),
        (front, pl.BlockSpec((KR, rows, width), lambda n: (0, 0, n))),
        (high, pl.BlockSpec((PW, width), lambda n: (0, n))),
        (low, pl.BlockSpec((PW, width), lambda n: (0, n))),
        (tok, ANY),
    ]
    more = {}
    if out is not None:
        ins.append((out, ANY))
        more["input_output_aliases"] = {len(ins) - 1: 0}
    return run(
        body,
        ins,
        [((KR, TB, KC * TB), F32, pl.BlockSpec((KR, rows, width), lambda n: (0, row // rows, n)))],
        [],
        grid=(KC * TB // width,),
        **more,
    )


class Plan:
    def __init__(self):
        self.steps = []

    def kernel(self, name, need, give, cost, call):
        self.steps.append((name, "kernel", need, give, cost, call))

    def permute(self, name, need, give, links, cost, call):
        self.steps.append((name, "permute", [need], [give], (links, cost), call))

    def order(self):
        ready, links = {}, {}
        todo = [s for s in self.steps if s[1] == "kernel"]
        moves = [s for s in self.steps if s[1] == "permute"]
        at, result = 0.0, []

        def move():
            nonlocal at
            for m in list(moves):
                if m[2][0] in ready:
                    moves.remove(m)
                    names, cost = m[4]
                    at += 1.0
                    begin = max([at] + [links.get(n, 0.0) for n in names])
                    for n in names:
                        links[n] = begin + cost
                    ready[m[3][0]] = begin + cost + 2.5
                    result.append(m)

        while todo or moves:
            move()
            known = [s for s in todo if all(n in ready for n in s[2])]
            best = min(known, key=lambda s: (max([at] + [ready[n] for n in s[2]]), todo.index(s)))
            todo.remove(best)
            at = max([at] + [ready[n] for n in best[2]]) + best[4]
            for n in best[3]:
                ready[n] = at
            result.append(best)
        self.end = at
        return result


def body(update_tiles, split_order, first_source, second_source, pivot_inverse):
    tiles = update_tiles.reshape(K, TB, TB)
    split, first, second = (x.reshape(LEVELS, K) for x in (split_order, first_source, second_source))
    cube, row_at, col = lax.axis_index("cube"), lax.axis_index("row"), lax.axis_index("col")
    x_at = (cube >> 1) & 3
    mask = (
        (cube & 1) * 64
        + (cube >> 3) * 32
        + row_at * 8
        + jnp.where((x_at == 1) | (x_at == 2), 4, 0)
        + jnp.where(x_at >= 2, 2, 0)
    )
    ids = jnp.stack([cube, row_at, col, mask]).astype(jnp.int32)
    lists = jnp.concatenate([split, first, second, jnp.roll(split, HALF, axis=1)], axis=0)

    def flip(axis, bits):
        return lambda v: lax.ppermute(v, axis, [(i, i ^ bits) for i in range(lax.axis_size(axis))])

    def toward(to):
        return lambda v: lax.ppermute(v, "row", [(0, to)])

    level_links = (("core",), ("xa",), ("xa", "xb"), ("y",))
    link_time = (3.5, 22.8, 22.8, 22.8)
    plan = Plan()
    kernel, permute = plan.kernel, plan.permute

    def level_steps(row, rows):
        n = f"c{row}"
        share = rows / 32
        kernel(f"{n}k0", [], [f"{n}s0"], 1.5 + 1.5 * share, lambda v, tok: first_send(row, rows, tiles, split, tok))
        for level in range(LEVELS):
            permute(f"{n}p{level}", f"{n}s{level}", f"{n}r{level}", level_links[level], link_time[level] * share, flip("cube", 1 << level))
            need = [f"{n}r{level}"] + ([f"{n}h{level}"] if level else [])
            if level < LEVELS - 1:
                kernel(
                    f"{n}k{level + 1}",
                    need,
                    [f"{n}s{level + 1}", f"{n}h{level + 1}"],
                    2 + 2 * share,
                    lambda v, tok, level=level: next_level(
                        level, row, rows, v[f"{n}h{level}"] if level else tiles, v[f"{n}r{level}"], split, first, second, tok
                    ),
                )
            else:
                kernel(
                    f"{n}k4",
                    need,
                    [f"{n}cols", f"{n}front"],
                    2 + 2 * share,
                    lambda v, tok, level=level: last_level(rows, v[f"{n}h3"], v[f"{n}r3"], first, second, tok),
                )
        permute(
            f"{n}pc",
            f"{n}cols",
            f"{n}sent",
            ("y2",),
            5.7 * share,
            lambda v: lax.ppermute(v, "col", [(0, 1)]),
        )

    def weight_steps():
        for level in range(LEVELS - 1, -1, -1):
            up = level + 1
            kernel(
                f"w{level}",
                [f"wo{up}", f"wr{up}"] if up < LEVELS else [],
                [f"wo{level}"],
                1.5,
                lambda v, tok, level=level, up=up: weights_back(level, v.get(f"wo{up}"), v.get(f"wr{up}"), ids, lists, tok),
            )
            permute(f"wp{level}", f"wo{level}", f"wr{level}", level_links[level], 1.0, flip("cube", 1 << level))

    def part_steps(index, row, rows):
        n = f"q{index}"
        m = rows / 128

        def add(name, terms, cuts, cost):
            kernel(
                f"{n}{name}", [f"{n}{t}" for t in terms], [f"{n}{name}{i}" for i in range(len(cuts))], cost,
                lambda v, tok: add_cut([v[f"{n}{t}"] for t in terms], cuts, rows, tok),
            )

        def move(name, what, axis, bits, links, cost):
            permute(f"{n}{name}", f"{n}{what}", f"{n}{name}", links, cost, flip(axis, bits))

        def join(name, pieces, cost):
            kernel(f"{n}{name}", [f"{n}{p}" for p in pieces], [f"{n}{name}"], cost, lambda v, tok: lay([v[f"{n}{p}"] for p in pieces], rows, tok))

        kernel(
            f"{n}t", ["wo0", "wr0"], [f"{n}keep", f"{n}send"], 3 + 10 * m,
            lambda v, tok: parts_of(row, rows, v["wo0"], v["wr0"], ids, lists, tiles, tok),
        )
        move("core", "send", "cube", 1, ("core",), 7 * m)
        add("a", ["keep", "core"], (32, 32), 1 + 4 * m)
        move("y", "a1", "cube", 8, ("y",), 45 * m)
        add("b", ["a0", "y"], (8, 8, 8, 8), 1 + 2 * m)
        for to in (1, 2, 3):
            permute(f"{n}z{to}", f"{n}b{to}", f"{n}z{to}", (("zp",), ("zp", "zm"), ("zm",))[to - 1], 11.4 * m, toward(to))
        add("c", ["b0", "z1", "z2", "z3"], (4, 4), 1.5)
        move("xa", "c1", "cube", 2, ("xa",), 5.7 * m)
        add("d", ["c0", "xa"], (2, 2), 1)
        move("xb", "d1", "cube", 6, ("xb",), 2.9 * m)
        add("e", ["d0", "xb"], (2,), 1)
        move("gb", "e0", "cube", 6, ("xb",), 2.9 * m)
        join("f", ["e0", "gb"], 1)
        move("ga", "f", "cube", 2, ("xa",), 5.7 * m)
        join("g", ["f", "ga"], 1)
        move("gy", "g", "cube", 8, ("y",), 11.4 * m)
        join("h", ["g", "gy"], 1.5)
        for bits in (1, 2, 3):
            move(f"gz{bits}", "h", "row", bits, (("zp",), ("zp", "zm"), ("zm",))[bits - 1], 23 * m)
        join("low", ["h", "gz1", "gz2", "gz3"], 1.5 + 4 * m)
        move("high", "low", "cube", 1, ("core",), 7 * m)
        last = index == len(PARTS) - 1
        kernel(
            f"{n}panel", [f"{n}low", f"{n}high"] + ([f"q{index - 1}panel"] if index else []),
            ["qh", "ql"] if last else [f"{n}panel"], 10,
            lambda v, tok: panel(row, rows, v[f"{n}low"], v[f"{n}high"], ids, pivot_inverse, v.get(f"q{index - 1}panel"), last, tok),
        )

    level_steps(*CHUNKS[0])
    weight_steps()
    for chunk in CHUNKS[1:]:
        level_steps(*chunk)
    for index, part in enumerate(PARTS):
        part_steps(index, *part)
    for index, (row, rows) in enumerate(CHUNKS):
        n = f"c{row}"
        kernel(
            f"{n}u", [f"{n}front", f"{n}cols", f"{n}sent", "qh", "ql"] + ([f"out{index - 1}"] if index else []), [f"out{index}"], 4,
            lambda v, tok, n=n, row=row, rows=rows, index=index: update(
                row, rows, v[f"{n}front"], v[f"{n}cols"], v[f"{n}sent"], ids, v["qh"], v["ql"], v.get(f"out{index - 1}"), tok
            ),
        )

    values = {}
    tok = ids
    for name, kind, need, give, _, call in plan.order():
        if kind == "kernel":
            results = call(values, tok)
            if not give[0].startswith("out"):
                tok = results[0]
            values.update(zip(give, results))
        else:
            values[give[0]] = call(values[need[0]])
    return values[f"out{len(CHUNKS) - 1}"].reshape(1, 1, 1, KR * TB, KC * TB)


def solution(mesh):
    return jax.shard_map(
        body,
        mesh=mesh,
        in_specs=(
            P("cube", "row", "col", None, None, None),
            P("cube", "row", "col", None, None),
            P("cube", "row", "col", None, None),
            P("cube", "row", "col", None, None),
            P(),
        ),
        out_specs=P("cube", "row", "col", None, None),
        check_vma=False,
    )
```

```python
import jax
import jax.numpy as jnp
from jax import lax
from jax.experimental import pallas as pl
from jax.experimental.pallas import tpu as pltpu
from jax.sharding import PartitionSpec as P

TB = 128
KR = 4
KC = 32
PW = 512
K = 128
HALF = 64
LEVELS = 4
F32 = jnp.float32
BF16 = jnp.bfloat16

GROUPS = ((0, 24, 4), (96, 16, 2))
CALLS = (1, 1)
ORDER = (
    "l0", "c0k0", "c72k0", "l1", "c0k1", "l2", "c72k1", "c48k0", "l3", "weight", "q0t", "q1t", "c72k2", "c48k1",
    "q0a", "c24k0", "c0k2", "c96k0", "q1a", "c48k2", "q0b", "c24k1", "q0c", "q0d", "c112k0", "c0k3", "q1b", "c96k1",
    "q0e", "q1c", "q0h", "q1d", "c24k2", "c96k2", "c0k4", "q1e", "c112k1", "q1h", "c24k3", "c48k3", "q0low",
    "c24k4", "c72k3", "inv", "q1low", "c48k4", "c112k2", "c96k3", "q0m", "c72k4", "c112k3", "q1m", "c96k4",
    "c112k4", "u0", "u1",
)
WORK = {
    "c0k1": 0.2, "c0k2": 0.8, "c0k4": 0.8, "l0": 0.2, "l1": 0.8, "l2": 0.05, "weight": 0.05, "c24k0": 0.1, "c24k1":
    0.1, "c24k2": 0.8, "c24k3": 0.8, "c24k4": 0.1, "c48k0": 0.1, "c48k1": 0.8, "c48k2": 0.4, "c48k3": 0.05, "c72k0":
    0.1, "c72k1": 0.4, "c72k2": 0.8, "c72k3": 0.8, "c96k0": 0.8, "c96k1": 0.2, "c96k2": 0.2, "c96k3": 0.8, "c96k4":
    0.4, "c112k1": 0.2, "c112k3": 0.8, "c112k4": 0.1, "q0a": 0.8, "q0b": 0.8, "q0d": 0.2, "q0e": 0.02, "q0m": 0.8,
    "q1a": 0.05, "q1b": 0.1, "q1d": 0.05, "q1e": 0.4, "q1h": 0.05, "q1low": 0.8, "q1m": 0.4, "inv": 0.8,
}
PARTS = ((0, 64), (64, 64))

ANY = pl.BlockSpec(memory_space=pl.ANY)
HBM = pl.BlockSpec(memory_space=pltpu.HBM)
SMEM = pl.BlockSpec(memory_space=pltpu.SMEM)
VMEM = pl.BlockSpec(memory_space=pltpu.VMEM)
DMA = pltpu.SemaphoreType.DMA


def nt(a, b):
    return lax.dot_general(a, b, (((1,), (1,)), ((), ())), preferred_element_type=F32)


def split2(x):
    high = x.astype(BF16)
    return high, (x - high.astype(F32)).astype(BF16)


FLOPS = [0]


def run(body, ins, outs, scratch, limit=32, **more):
    return pl.pallas_call(
        body,
        in_specs=[s for _, s in ins],
        out_specs=[ANY if s is HBM else s for _, _, s in outs],
        out_shape=[pltpu.HBM(s, d) if spec is HBM else jax.ShapeDtypeStruct(s, d) for s, d, spec in outs],
        scratch_shapes=scratch,
        compiler_params=pltpu.CompilerParams(vmem_limit_bytes=limit << 20),
        cost_estimate=pl.CostEstimate(flops=FLOPS[0], bytes_accessed=0, transcendentals=0),
        **more,
    )(*[a for a, _ in ins])


def first_split(row, rows, tiles, split, tok):
    def body(split_ref, tiles_ref, _, send_ref, keep_ref, pool, buf, sem):
        get = pltpu.make_async_copy(tiles_ref.at[:, pl.ds(row, rows), :], pool, sem.at[0])
        get.start()
        get.wait()

        def step(i, c):
            buf[i] = pool[split_ref[0, i]]
            return c

        lax.fori_loop(0, HALF, step, 0, unroll=8)
        one = pltpu.make_async_copy(buf.at[pl.ds(0, HALF)], send_ref, sem.at[1])
        one.start()
        lax.fori_loop(HALF, K, step, 0, unroll=8)
        two = pltpu.make_async_copy(buf.at[pl.ds(HALF, HALF)], keep_ref, sem.at[2])
        two.start()
        one.wait()
        two.wait()

    return run(
        body,
        [(split, SMEM), (tiles, ANY), (tok, ANY)],
        [((HALF, rows, TB), F32, ANY)] * 2,
        [pltpu.VMEM((K, rows, TB), F32), pltpu.VMEM((K, rows, TB), F32), DMA((3,))],
    )


def fetch(kept_ref, recv_ref, pool, sem):
    one = pltpu.make_async_copy(kept_ref, pool.at[pl.ds(0, HALF)], sem.at[0])
    two = pltpu.make_async_copy(recv_ref, pool.at[pl.ds(HALF, HALF)], sem.at[1])
    one.start()
    two.start()
    one.wait()
    two.wait()


def next_level(level, rows, kept, recv, split, first, second, tok):
    def body(split_ref, first_ref, second_ref, kept_ref, recv_ref, _, send_ref, keep_ref, pool, buf, sem):
        fetch(kept_ref, recv_ref, pool, sem)

        def step(i, c):
            t = split_ref[level + 1, i]
            buf[i] = pool[first_ref[level, t]] + pool[second_ref[level, t]]
            return c

        lax.fori_loop(0, HALF, step, 0, unroll=8)
        one = pltpu.make_async_copy(buf.at[pl.ds(0, HALF)], send_ref, sem.at[2])
        one.start()
        lax.fori_loop(HALF, K, step, 0, unroll=8)
        two = pltpu.make_async_copy(buf.at[pl.ds(HALF, HALF)], keep_ref, sem.at[3])
        two.start()
        one.wait()
        two.wait()

    return run(
        body,
        [(split, SMEM), (first, SMEM), (second, SMEM), (kept, ANY), (recv, ANY), (tok, ANY)],
        [((HALF, rows, TB), F32, ANY)] * 2,
        [pltpu.VMEM((K, rows, TB), F32), pltpu.VMEM((K, rows, TB), F32), DMA((4,))],
    )


def last_level(index, count, rows, kept, recv, first, second, before, tok):
    def body(first_ref, second_ref, kept_ref, recv_ref, *refs):
        cols_ref, front_ref, pool, buf, cbuf, sem = refs[-6:]
        level = LEVELS - 1
        fetch(kept_ref, recv_ref, pool, sem)
        for i in range(KR):
            for j in range(PW // TB):
                t = i * KC + j
                tile = pool[first_ref[level, t]] + pool[second_ref[level, t]]
                buf[i, :, j * TB:(j + 1) * TB] = tile
                cbuf[i, :, j * TB:(j + 1) * TB] = tile
        one = pltpu.make_async_copy(cbuf, cols_ref.at[index], sem.at[2])
        one.start()
        for i in range(KR):

            def step(j, c):
                t = i * KC + j
                at = pl.ds(pl.multiple_of(j * TB, TB), TB)
                buf[i, :, at] = pool[first_ref[level, t]] + pool[second_ref[level, t]]
                return c

            lax.fori_loop(PW // TB, KC, step, 0, unroll=4)
        two = pltpu.make_async_copy(buf, front_ref, sem.at[3])
        two.start()
        one.wait()
        two.wait()

    ins = [(first, SMEM), (second, SMEM), (kept, ANY), (recv, ANY), (tok, ANY)]
    more = {}
    if before is not None:
        ins.append((before, ANY))
        more["input_output_aliases"] = {len(ins) - 1: 0}
    return run(
        body,
        ins,
        [((count, KR, rows, PW), F32, ANY), ((KR, rows, KC * TB), F32, HBM)],
        [
            pltpu.VMEM((K, rows, TB), F32),
            pltpu.VMEM((KR, rows, KC * TB), F32),
            pltpu.VMEM((KR, rows, PW), F32),
            DMA((4,)),
        ],
        **more,
    )


def flips(bits):
    return ((bits >> 1) & 1) + ((bits >> 2) & 1) * 2 + ((bits >> 3) & 1) * 4 + (bits & 1) * 8


def own_lists(split, first, second, tok):
    def body(split_ref, first_ref, second_ref, _, out_ref):
        out_ref[0, 0:4, :] = split_ref[...]
        out_ref[0, 4:8, :] = first_ref[...]
        out_ref[0, 8:12, :] = second_ref[...]
        order = split_ref[...]
        out_ref[0, 12:16, :] = jnp.concatenate([order[:, HALF:], order[:, :HALF]], axis=1)

    return run(body, [(split, VMEM), (first, VMEM), (second, VMEM), (tok, ANY)], [((1, 16, K), jnp.int32, VMEM)], [])


def weights(ids, near, far, tok):
    def body(ids_ref, near_ref, far_ref, _, out_ref, lists_ref):
        lists_ref[0:8] = near_ref[...]
        lists_ref[8:16] = far_ref[...]
        cube = ids_ref[0]
        row = lax.broadcasted_iota(jnp.int32, (K, K), 0)
        lane = lax.broadcasted_iota(jnp.int32, (K, K), 1)
        mine = jnp.logical_and(lane == jnp.bitwise_xor(row, ids_ref[3]), ids_ref[1] == 0)
        weight = jnp.where(mine, 1.0, 0.0).astype(BF16)
        for level in range(LEVELS - 1, -1, -1):
            parent = lists_ref[flips(cube & ((2 << level) - 1))]
            child = lists_ref[flips(cube & ((1 << level) - 1))]
            one = jnp.where(row == parent[4 + level:5 + level, :], 1.0, 0.0)
            two = jnp.where(row == parent[8 + level:9 + level, :], 1.0, 0.0)
            joined = nt(weight, (one + two).astype(BF16))
            bit = (cube >> level) & 1
            joined = jnp.where((lane >> 6) == bit, joined, 0.0).astype(BF16)
            order = jnp.where(row == child[12 + level:13 + level, :], 1.0, 0.0).astype(BF16)
            weight = nt(joined, order).astype(BF16)
        out_ref[...] = weight.astype(F32)

    return run(
        body,
        [(ids, SMEM), (near, VMEM), (far, VMEM), (tok, ANY)],
        [((K, K), F32, VMEM)],
        [pltpu.VMEM((16, 16, K), jnp.int32)],
    )


def parts_of(row, rows, weight, tiles, tok):
    def body(weight_ref, tiles_ref, _, keep_ref, send_ref, pool, buf, sem):
        get = pltpu.make_async_copy(tiles_ref.at[:, pl.ds(row, rows), :], pool, sem.at[0])
        get.start()
        w = weight_ref[...].astype(BF16)
        w = jnp.concatenate([w, w], axis=1)
        get.wait()
        flat = pool.reshape(K * rows, TB)
        out = buf.reshape(K * rows, TB)

        def step(n, carry):
            at = n * 2
            x = jnp.concatenate(
                [flat[pl.ds(at, K, stride=rows), :], flat[pl.ds(at + 1, K, stride=rows), :]], axis=1
            )
            y = jnp.dot(w, jnp.concatenate(split2(x), axis=0), preferred_element_type=F32)
            out[pl.ds(at, K, stride=rows), :] = y[:, :TB]
            out[pl.ds(at + 1, K, stride=rows), :] = y[:, TB:]
            return carry

        lax.fori_loop(0, rows // 2, step, 0, unroll=4)
        one = pltpu.make_async_copy(buf.at[pl.ds(0, HALF)], keep_ref, sem.at[1])
        two = pltpu.make_async_copy(buf.at[pl.ds(HALF, HALF)], send_ref, sem.at[2])
        one.start()
        two.start()
        one.wait()
        two.wait()

    return run(
        body,
        [(weight, VMEM), (tiles, ANY), (tok, ANY)],
        [((HALF, rows, TB), F32, ANY)] * 2,
        [pltpu.VMEM((K, rows, TB), F32), pltpu.VMEM((K, rows, TB), F32), DMA((3,))],
    )


def add_cut(terms, cuts, rows, tok):
    def body(*refs):
        total = refs[0][...]
        for term in refs[1:len(terms)]:
            total = total + term[...]
        at = 0
        for cut, ref in zip(cuts, refs[len(terms) + 1:]):
            ref[...] = total[at:at + cut]
            at += cut

    return run(
        body, [(t, VMEM) for t in terms] + [(tok, ANY)], [((cut, rows, TB), F32, VMEM) for cut in cuts], []
    )


def lay(pieces, rows, tok):
    count = sum(p.shape[0] for p in pieces)

    def body(*refs):
        out_ref, sem = refs[-2:]
        copies = []
        at = 0
        for n, piece in enumerate(pieces):
            copies.append(
                pltpu.make_async_copy(refs[n], out_ref.at[pl.ds(at, piece.shape[0])], sem.at[n])
            )
            at += piece.shape[0]
        for copy in copies:
            copy.start()
        for copy in copies:
            copy.wait()

    return run(
        body, [(p, ANY) for p in pieces] + [(tok, ANY)], [((count, rows, TB), pieces[0].dtype, ANY)], [DMA((len(pieces),))]
    )


def prepare(rows, low, high, ids, tok):
    def body(ids_ref, low_ref, high_ref, _, top_ref, rest_ref, pool, sem):
        one = pltpu.make_async_copy(low_ref, pool.at[pl.ds(0, HALF)], sem.at[0])
        two = pltpu.make_async_copy(high_ref, pool.at[pl.ds(HALF, HALF)], sem.at[1])
        one.start()
        two.start()
        mask = ids_ref[4]
        one.wait()
        two.wait()
        for i in range(KR):

            def step(j, c):
                at = pl.ds(pl.multiple_of(j * TB, TB), TB)
                h, lo = split2(pool[jnp.bitwise_xor(i * KC + j, mask)])
                top_ref[i * rows:(i + 1) * rows, at] = h
                rest_ref[i * rows:(i + 1) * rows, at] = lo
                return c

            lax.fori_loop(0, KC, step, 0, unroll=4)

    return run(
        body,
        [(ids, SMEM), (low, ANY), (high, ANY), (tok, ANY)],
        [((KR * rows, KC * TB), BF16, VMEM)] * 2,
        [pltpu.VMEM((K, rows, TB), F32), DMA((2,))],
    )


def arrange(inverse, tok):
    def body(inv_ref, _, top_ref, rest_ref):
        pieces = [inv_ref[:, i * TB + row:i * TB + row + n] for row, n in PARTS for i in range(KR)]
        top_ref[...], rest_ref[...] = split2(jnp.concatenate(pieces, axis=1))

    return run(body, [(inverse, VMEM), (tok, ANY)], [((PW, PW), BF16, VMEM)] * 2, [])


def update(groups, cols, sent, fronts, ids, inverse, pivots, out, tok):
    width = 512
    chunks = [(top + n * rows, rows) for top, rows, count in groups for n in range(count)]
    first = chunks[0][0]
    tall = sum(rows for _, rows in chunks)
    m = KR * tall
    at_pivots = 4 + 2 * len(groups)
    at_fronts = at_pivots + len(pivots)

    def body(ids_ref, inv_ref, low_ref, *refs):
        out_ref, left = refs[-2:]
        refs = (ids_ref, inv_ref, low_ref, None) + refs

        @pl.when(pl.program_id(0) == 0)
        def _():
            at = 0
            for n, (_, rows, count) in enumerate(groups):
                size = KR * rows * count
                own, other = refs[4 + 2 * n], refs[5 + 2 * n]
                h, lo = split2(jnp.where(ids_ref[2] == 0, own[...], other[...]).reshape(size, PW))
                both = jnp.dot(jnp.concatenate([h, lo], axis=0), inv_ref[...], preferred_element_type=F32)
                total = both[:size] + both[size:] + jnp.dot(h, low_ref[...], preferred_element_type=F32)
                left[at:at + size, :], left[m + at:m + at + size, :] = split2(total)
                at += size

        at, total = 0, 0.0
        for n, (_, size) in enumerate(PARTS):
            h = left[:, at:at + KR * size]
            both = jnp.dot(h, refs[at_pivots + 2 * n][...], preferred_element_type=F32)
            total += both[:m] + both[m:] + jnp.dot(h[:m], refs[at_pivots + 2 * n + 1][...], preferred_element_type=F32)
            at += KR * size
        at = 0
        for n, (row, rows) in enumerate(chunks):
            one = total[at:at + KR * rows].reshape(KR, rows, width)
            out_ref[:, row - first:row - first + rows, :] = refs[at_fronts + n][...] - one
            at += KR * rows

    square = pl.BlockSpec((PW, PW), lambda n: (0, 0))
    ins = [(ids, SMEM), (inverse[0], square), (inverse[1], square)]
    for (_, rows, count), own, other in zip(groups, cols, sent):
        pivot = pl.BlockSpec((count, KR, rows, PW), lambda n: (0, 0, 0, 0))
        ins += [(own, pivot), (other, pivot)]
    ins += [(p, pl.BlockSpec((p.shape[0], width), lambda n: (0, n))) for p in pivots]
    ins += [(f, pl.BlockSpec((KR, f.shape[1], width), lambda n: (0, 0, n))) for f in fronts]
    ins.append((tok, ANY))
    more = {}
    if out is not None:
        ins.append((out, ANY))
        more["input_output_aliases"] = {len(ins) - 1: 0}
    return run(
        body,
        ins,
        [((KR, TB, KC * TB), F32, pl.BlockSpec((KR, tall, width), lambda n: (0, first // tall, n)))],
        [pltpu.VMEM((2 * m, PW), BF16)],
        limit=56,
        grid=(KC * TB // width,),
        **more,
    )


class Plan:
    def __init__(self):
        self.steps = []
        self.log = []

    def kernel(self, name, need, give, cost, call):
        self.steps.append((name, "kernel", need, give, cost, call))

    def permute(self, name, need, give, links, cost, call):
        self.steps.append((name, "permute", [need], [give], (links, cost), call))

    def emit(self):
        kernels = {s[0]: s for s in self.steps if s[1] == "kernel"}
        names = ORDER or [s[0] for s in self.order() if s[1] == "kernel"]
        for name in names:
            yield kernels[name]
            for s in self.steps:
                if s[1] == "permute" and s[2][0] in kernels[name][3]:
                    yield s

    def order(self, limit=5):
        ready, links, flying = {}, {}, set()
        todo = [s for s in self.steps if s[1] == "kernel"]
        moves = {}
        for s in self.steps:
            if s[1] == "permute":
                moves.setdefault(s[2][0], []).append(s)
        at, result = 0.0, []
        while todo:
            known = [s for s in todo if all(n in ready for n in s[2])]
            fits = [
                s for s in known
                if len(flying - set(s[2])) + sum(len(moves.get(n, ())) for n in s[3]) <= limit
            ] or known
            best = min(fits, key=lambda s: (max([at] + [ready[n] for n in s[2]]), todo.index(s)))
            todo.remove(best)
            at = max([at] + [ready[n] for n in best[2]]) + best[4]
            self.log.append((round(at, 1), best[0]))
            result.append(best)
            flying -= set(best[2])
            for n in best[3]:
                ready[n] = at
                for m in moves.get(n, ()):
                    names, cost = m[4]
                    at += 1.5
                    begin = max([at] + [links.get(x, 0.0) for x in names])
                    for x in names:
                        links[x] = begin + cost
                    ready[m[3][0]] = begin + cost + 2.0
                    flying.add(m[3][0])
                    result.append(m)
        self.end = at
        return result


def flip(axis, bits):
    return lambda v: lax.ppermute(v, axis, [(i, i ^ bits) for i in range(lax.axis_size(axis))])


def make_plan(tiles, split, first, second, ids, pivot_inverse):
    level_links = (("core",), ("xa",), ("xa", "xb"), ("y",))
    link_time = (3.5, 22.8, 22.8, 22.8)
    plan = Plan()
    kernel, permute = plan.kernel, plan.permute

    def level_steps(group, index):
        top, rows, count = group
        row = top + index * rows
        n, g = f"c{row}", f"g{top}"
        share = rows / 32
        kernel(f"{n}k0", [], [f"{n}s0", f"{n}h0"], 0.6 + 0.4 * share, lambda v, tok: first_split(row, rows, tiles, split, tok))
        for level in range(LEVELS):
            permute(f"{n}p{level}", f"{n}s{level}", f"{n}r{level}", level_links[level], link_time[level] * share, flip("cube", 1 << level))
            need = [f"{n}r{level}", f"{n}h{level}"]
            if level < LEVELS - 1:
                kernel(
                    f"{n}k{level + 1}",
                    need,
                    [f"{n}s{level + 1}", f"{n}h{level + 1}"],
                    0.8 + 0.9 * share,
                    lambda v, tok, level=level: next_level(
                        level, rows, v[f"{n}h{level}"], v[f"{n}r{level}"], split, first, second, tok
                    ),
                )
            else:
                kernel(
                    f"{n}k4",
                    need + ([f"{g}cols{index - 1}"] if index else []),
                    [f"{g}cols{index}", f"{n}front"],
                    0.8 + 0.9 * share,
                    lambda v, tok: last_level(
                        index, count, rows, v[f"{n}h3"], v[f"{n}r3"], first, second, v.get(f"{g}cols{index - 1}"), tok
                    ),
                )
        if index == count - 1:
            permute(
                f"{g}pc", f"{g}cols{index}", f"{g}sent", ("y2",), 5.7 * share * count,
                lambda v: lax.ppermute(v, "col", [(0, 1)]),
            )

    def part_steps(index, row, rows):
        n = f"q{index}"
        m = rows / 128

        def add(name, terms, cuts, cost):
            kernel(
                f"{n}{name}", [f"{n}{t}" for t in terms], [f"{n}{name}{i}" for i in range(len(cuts))], cost,
                lambda v, tok: add_cut([v[f"{n}{t}"] for t in terms], cuts, rows, tok),
            )

        def move(name, what, axis, bits, links, cost):
            permute(f"{n}{name}", f"{n}{what}", f"{n}{name}", links, cost, flip(axis, bits))

        def join(name, pieces, cost):
            kernel(f"{n}{name}", [f"{n}{p}" for p in pieces], [f"{n}{name}"], cost, lambda v, tok: lay([v[f"{n}{p}"] for p in pieces], rows, tok))

        kernel(f"{n}t", ["weight"], [f"{n}keep", f"{n}send"], 2 + 6 * m, lambda v, tok: parts_of(row, rows, v["weight"], tiles, tok))
        move("core", "send", "cube", 1, ("core",), 7 * m)
        add("a", ["keep", "core"], (64,), 0.5 + 2 * m)
        permute(f"{n}zs", f"{n}a0", f"{n}zs", ("gather",), 16 + 30 * m, lambda v: lax.psum_scatter(v, "row", tiled=True))
        add("b", ["zs"], (8, 8), 0.5 + m)
        move("y", "b1", "cube", 8, ("y",), 11.4 * m)
        add("c", ["b0", "y"], (8,), 0.5)
        move("xa", "c0", "cube", 2, ("xa",), 11.4 * m)
        add("d", ["c0", "xa"], (8,), 0.5)
        move("xb", "d0", "cube", 6, ("xb",), 11.4 * m)
        add("e", ["d0", "xb"], (8,), 0.5)
        move("gy", "e0", "cube", 8, ("y",), 11.4 * m)
        join("h", ["e0", "gy"], 1)
        permute(f"{n}gz", f"{n}h", f"{n}gz", ("gather",), 16 + 30 * m, lambda v: lax.all_gather(v, "row", tiled=True))
        join("low", ["gz"], 1 + 2 * m)
        move("high", "low", "cube", 1, ("core",), 7 * m)
        kernel(f"{n}m", [f"{n}low", f"{n}high"], [f"{n}m0", f"{n}m1"], 4, lambda v, tok: prepare(rows, v[f"{n}low"], v[f"{n}high"], ids, tok))

    level_steps(GROUPS[0], 0)
    kernel("l0", [], ["ls0"], 0.6, lambda v, tok: own_lists(split, first, second, tok))
    for n, bits in enumerate((2, 4, 8, 1)):
        permute(f"lp{n}", f"ls{n}", f"lr{n}", level_links[(1, 2, 3, 0)[n]], 0.2, flip("cube", bits))
        if n < 3:
            kernel(f"l{n + 1}", [f"ls{n}", f"lr{n}"], [f"ls{n + 1}"], 0.5, lambda v, tok, n=n: lay([v[f"ls{n}"], v[f"lr{n}"]], 16, tok))
    kernel("weight", ["ls3", "lr3"], ["weight"], 1.5, lambda v, tok: weights(ids, v["ls3"], v["lr3"], tok))
    for group in GROUPS:
        for index in range(group[2]):
            if group is not GROUPS[0] or index:
                level_steps(group, index)
    for index, part in enumerate(PARTS):
        part_steps(index, *part)
    kernel("inv", [], ["inv0", "inv1"], 2, lambda v, tok: arrange(pivot_inverse, tok))
    pivots = [f"q{i}m{j}" for i in range(len(PARTS)) for j in range(2)]
    start = 0
    for at, number in enumerate(CALLS):
        groups = GROUPS[start:start + number]
        start += number
        cols = [f"g{top}cols{count - 1}" for top, rows, count in groups]
        sent = [f"g{top}sent" for top, rows, count in groups]
        fronts = [f"c{top + n * rows}front" for top, rows, count in groups for n in range(count)]
        kernel(
            f"u{at}", fronts + cols + sent + pivots + ["inv0", "inv1"] + ([f"out{at - 1}"] if at else []), [f"out{at}"], 8,
            lambda v, tok, at=at, groups=groups, names=(cols, sent, fronts): update(
                groups, *[[v[n] for n in x] for x in names], ids, (v["inv0"], v["inv1"]), [v[p] for p in pivots], v.get(f"out{at - 1}"), tok
            ),
        )

    return plan


def body(update_tiles, split_order, first_source, second_source, pivot_inverse):
    tiles = pltpu.with_memory_space_constraint(update_tiles.reshape(K, TB, TB), pltpu.HBM)
    split, first, second = (x.reshape(LEVELS, K) for x in (split_order, first_source, second_source))
    cube, row_at, col = lax.axis_index("cube"), lax.axis_index("row"), lax.axis_index("col")
    mask = (cube & 1) * 64 + row_at * 16 + (cube >> 3) * 8
    ids = jnp.stack([cube, row_at, col, mask, mask - row_at * 16]).astype(jnp.int32)
    plan = make_plan(tiles, split, first, second, ids, pivot_inverse)
    values = {}
    tok = ids
    for name, kind, need, give, cost, call in plan.emit():
        if kind == "kernel":
            FLOPS[0] = int(WORK.get(name, 0) * 2.2e10)
            with jax.named_scope(name):
                results = call(values, tok)
            if not give[0].startswith("out"):
                tok = results[0]
            values.update(zip(give, results))
        else:
            with jax.named_scope(name):
                values[give[0]] = call(values[need[0]])
    return values[f"out{len(CALLS) - 1}"].reshape(1, 1, 1, KR * TB, KC * TB)


def solution(mesh):
    return jax.shard_map(
        body,
        mesh=mesh,
        in_specs=(
            P("cube", "row", "col", None, None, None),
            P("cube", "row", "col", None, None),
            P("cube", "row", "col", None, None),
            P("cube", "row", "col", None, None),
            P(),
        ),
        out_specs=P("cube", "row", "col", None, None),
        check_vma=False,
    )
```

```python
import jax
import jax.numpy as jnp
from jax import lax
from jax.experimental import pallas as pl
from jax.experimental.pallas import tpu as pltpu
from jax.sharding import PartitionSpec as P

TB = 128
KR = 4
KC = 32
PW = 512
K = 128
HALF = 64
LEVELS = 4
F32 = jnp.float32
BF16 = jnp.bfloat16

GROUPS = ((0, 24, 2), (48, 24, 2), (96, 16, 1), (112, 16, 1))
CALLS = (2, 2)
ORDER = (
    5, 0, 6, 25, 7, 10, 8, 26, 9, 35, 44, 1, 36, 27, 20, 15, 45, 11, 30, 2, 12, 16, 21, 37, 38, 3, 39, 31, 46, 47,
    17, 48, 40, 41, 49, 22, 53, 50, 13, 18, 4, 14, 42, 23, 19, 32, 51, 24, 28, 33, 43, 52, 54, 34, 29, 55,
)
WORK = {
    0: 0.2, 2: 0.2, 3: 0.1, 4: 0.8, 5: 0.1, 6: 0.02, 7: 0.2, 8: 0.02, 9: 0.4, 10: 0.4, 11: 0.05, 13: 0.8, 15: 0.8,
    16: 0.4, 18: 0.2, 19: 0.05, 20: 0.8, 22: 0.8, 23: 0.8, 24: 0.1, 26: 0.1, 27: 0.8, 28: 0.8, 29: 0.2, 31: 0.8, 32:
    0.1, 33: 0.8, 34: 0.8, 36: 0.4, 37: 0.2, 38: 0.2, 40: 0.2, 41: 0.2, 43: 0.4, 44: 0.8, 46: 0.2, 47: 0.1, 48: 0.8,
    49: 0.05, 55: 0.4,
}
PARTS = ((0, 64), (64, 64))

ANY = pl.BlockSpec(memory_space=pl.ANY)
HBM = pl.BlockSpec(memory_space=pltpu.HBM)
SMEM = pl.BlockSpec(memory_space=pltpu.SMEM)
VMEM = pl.BlockSpec(memory_space=pltpu.VMEM)
DMA = pltpu.SemaphoreType.DMA


def nt(a, b):
    return lax.dot_general(a, b, (((1,), (1,)), ((), ())), preferred_element_type=F32)


def split2(x):
    high = x.astype(BF16)
    return high, (x - high.astype(F32)).astype(BF16)


FLOPS = [0]


def run(body, ins, outs, scratch, limit=16, **more):
    return pl.pallas_call(
        body,
        in_specs=[ANY if s is HBM else s for _, s in ins],
        out_specs=[ANY if s is HBM else s for _, _, s in outs],
        out_shape=[pltpu.HBM(s, d) if spec is HBM else jax.ShapeDtypeStruct(s, d) for s, d, spec in outs],
        scratch_shapes=scratch,
        compiler_params=pltpu.CompilerParams(vmem_limit_bytes=limit << 20),
        cost_estimate=pl.CostEstimate(flops=FLOPS[0], bytes_accessed=0, transcendentals=0),
        **more,
    )(*[pltpu.with_memory_space_constraint(a, pltpu.HBM) if s is HBM else a for a, s in ins])


def first_split(row, rows, tiles, split, tok):
    def body(split_ref, tiles_ref, _, send_ref, keep_ref, pool, buf, sem):
        get = pltpu.make_async_copy(tiles_ref.at[:, pl.ds(row, rows), :], pool, sem.at[0])
        get.start()
        get.wait()

        def step(i, c):
            buf[i] = pool[split_ref[0, i]]
            return c

        lax.fori_loop(0, HALF, step, 0, unroll=8)
        one = pltpu.make_async_copy(buf.at[pl.ds(0, HALF)], send_ref, sem.at[1])
        one.start()
        lax.fori_loop(HALF, K, step, 0, unroll=8)
        two = pltpu.make_async_copy(buf.at[pl.ds(HALF, HALF)], keep_ref, sem.at[2])
        two.start()
        one.wait()
        two.wait()

    return run(
        body,
        [(split, SMEM), (tiles, ANY), (tok, ANY)],
        [((HALF, rows, TB), F32, ANY), ((HALF, rows, TB), F32, HBM)],
        [pltpu.VMEM((K, rows, TB), F32), pltpu.VMEM((K, rows, TB), F32), DMA((3,))],
    )


def fetch(kept_ref, recv_ref, pool, sem):
    one = pltpu.make_async_copy(kept_ref, pool.at[pl.ds(0, HALF)], sem.at[0])
    two = pltpu.make_async_copy(recv_ref, pool.at[pl.ds(HALF, HALF)], sem.at[1])
    one.start()
    two.start()
    one.wait()
    two.wait()


def next_level(level, rows, kept, recv, split, first, second, tok):
    def body(split_ref, first_ref, second_ref, kept_ref, recv_ref, _, send_ref, keep_ref, pool, buf, sem):
        fetch(kept_ref, recv_ref, pool, sem)

        def step(i, c):
            t = split_ref[level + 1, i]
            buf[i] = pool[first_ref[level, t]] + pool[second_ref[level, t]]
            return c

        lax.fori_loop(0, HALF, step, 0, unroll=8)
        one = pltpu.make_async_copy(buf.at[pl.ds(0, HALF)], send_ref, sem.at[2])
        one.start()
        lax.fori_loop(HALF, K, step, 0, unroll=8)
        two = pltpu.make_async_copy(buf.at[pl.ds(HALF, HALF)], keep_ref, sem.at[3])
        two.start()
        one.wait()
        two.wait()

    return run(
        body,
        [(split, SMEM), (first, SMEM), (second, SMEM), (kept, HBM), (recv, ANY), (tok, ANY)],
        [((HALF, rows, TB), F32, ANY), ((HALF, rows, TB), F32, HBM)],
        [pltpu.VMEM((K, rows, TB), F32), pltpu.VMEM((K, rows, TB), F32), DMA((4,))],
    )


def last_level(index, count, rows, kept, recv, first, second, before, tok):
    def body(first_ref, second_ref, kept_ref, recv_ref, *refs):
        cols_ref, front_ref, pool, buf, cbuf, sem = refs[-6:]
        level = LEVELS - 1
        fetch(kept_ref, recv_ref, pool, sem)
        for i in range(KR):
            for j in range(PW // TB):
                t = i * KC + j
                tile = pool[first_ref[level, t]] + pool[second_ref[level, t]]
                buf[i, :, j * TB:(j + 1) * TB] = tile
                cbuf[i, :, j * TB:(j + 1) * TB] = tile
        one = pltpu.make_async_copy(cbuf, cols_ref.at[index], sem.at[2])
        one.start()
        for i in range(KR):

            def step(j, c):
                t = i * KC + j
                at = pl.ds(pl.multiple_of(j * TB, TB), TB)
                buf[i, :, at] = pool[first_ref[level, t]] + pool[second_ref[level, t]]
                return c

            lax.fori_loop(PW // TB, KC, step, 0, unroll=4)
        two = pltpu.make_async_copy(buf, front_ref, sem.at[3])
        two.start()
        one.wait()
        two.wait()

    ins = [(first, SMEM), (second, SMEM), (kept, HBM), (recv, ANY), (tok, ANY)]
    more = {}
    if before is not None:
        ins.append((before, ANY))
        more["input_output_aliases"] = {len(ins) - 1: 0}
    return run(
        body,
        ins,
        [((count, KR, rows, PW), F32, ANY), ((KR, rows, KC * TB), F32, HBM)],
        [
            pltpu.VMEM((K, rows, TB), F32),
            pltpu.VMEM((KR, rows, KC * TB), F32),
            pltpu.VMEM((KR, rows, PW), F32),
            DMA((4,)),
        ],
        **more,
    )


def flips(bits):
    return ((bits >> 1) & 1) + ((bits >> 2) & 1) * 2 + ((bits >> 3) & 1) * 4 + (bits & 1) * 8


def own_lists(split, first, second, tok):
    def body(split_ref, first_ref, second_ref, _, out_ref):
        out_ref[0, 0:4, :] = split_ref[...]
        out_ref[0, 4:8, :] = first_ref[...]
        out_ref[0, 8:12, :] = second_ref[...]
        order = split_ref[...]
        out_ref[0, 12:16, :] = jnp.concatenate([order[:, HALF:], order[:, :HALF]], axis=1)

    return run(body, [(split, VMEM), (first, VMEM), (second, VMEM), (tok, ANY)], [((1, 16, K), jnp.int32, VMEM)], [])


def weights(ids, near, far, tok):
    def body(ids_ref, near_ref, far_ref, _, out_ref, lists_ref):
        lists_ref[0:8] = near_ref[...]
        lists_ref[8:16] = far_ref[...]
        cube = ids_ref[0]
        row = lax.broadcasted_iota(jnp.int32, (K, K), 0)
        lane = lax.broadcasted_iota(jnp.int32, (K, K), 1)
        mine = jnp.logical_and(lane == jnp.bitwise_xor(row, ids_ref[3]), ids_ref[1] == 0)
        weight = jnp.where(mine, 1.0, 0.0).astype(BF16)
        for level in range(LEVELS - 1, -1, -1):
            parent = lists_ref[flips(cube & ((2 << level) - 1))]
            child = lists_ref[flips(cube & ((1 << level) - 1))]
            one = jnp.where(row == parent[4 + level:5 + level, :], 1.0, 0.0)
            two = jnp.where(row == parent[8 + level:9 + level, :], 1.0, 0.0)
            joined = nt(weight, (one + two).astype(BF16))
            bit = (cube >> level) & 1
            joined = jnp.where((lane >> 6) == bit, joined, 0.0).astype(BF16)
            order = jnp.where(row == child[12 + level:13 + level, :], 1.0, 0.0).astype(BF16)
            weight = nt(joined, order).astype(BF16)
        out_ref[...] = weight.astype(F32)

    return run(
        body,
        [(ids, SMEM), (near, VMEM), (far, VMEM), (tok, ANY)],
        [((K, K), F32, VMEM)],
        [pltpu.VMEM((16, 16, K), jnp.int32)],
    )


def parts_of(row, rows, weight, tiles, tok):
    def body(weight_ref, tiles_ref, _, keep_ref, send_ref, pool, buf, sem):
        get = pltpu.make_async_copy(tiles_ref.at[:, pl.ds(row, rows), :], pool, sem.at[0])
        get.start()
        w = weight_ref[...].astype(BF16)
        w = jnp.concatenate([w, w], axis=1)
        get.wait()
        flat = pool.reshape(K * rows, TB)
        out = buf.reshape(K * rows, TB)

        def step(n, carry):
            at = n * 2
            x = jnp.concatenate(
                [flat[pl.ds(at, K, stride=rows), :], flat[pl.ds(at + 1, K, stride=rows), :]], axis=1
            )
            y = jnp.dot(w, jnp.concatenate(split2(x), axis=0), preferred_element_type=F32)
            out[pl.ds(at, K, stride=rows), :] = y[:, :TB]
            out[pl.ds(at + 1, K, stride=rows), :] = y[:, TB:]
            return carry

        lax.fori_loop(0, rows // 2, step, 0, unroll=4)
        one = pltpu.make_async_copy(buf.at[pl.ds(0, HALF)], keep_ref, sem.at[1])
        two = pltpu.make_async_copy(buf.at[pl.ds(HALF, HALF)], send_ref, sem.at[2])
        one.start()
        two.start()
        one.wait()
        two.wait()

    return run(
        body,
        [(weight, VMEM), (tiles, ANY), (tok, ANY)],
        [((HALF, rows, TB), F32, ANY)] * 2,
        [pltpu.VMEM((K, rows, TB), F32), pltpu.VMEM((K, rows, TB), F32), DMA((3,))],
    )


def add_cut(terms, cuts, rows, tok):
    def body(*refs):
        total = refs[0][...]
        for term in refs[1:len(terms)]:
            total = total + term[...]
        at = 0
        for cut, ref in zip(cuts, refs[len(terms) + 1:]):
            ref[...] = total[at:at + cut]
            at += cut

    return run(
        body, [(t, VMEM) for t in terms] + [(tok, ANY)], [((cut, rows, TB), F32, VMEM) for cut in cuts], []
    )


def lay(pieces, rows, tok):
    count = sum(p.shape[0] for p in pieces)

    def body(*refs):
        out_ref, sem = refs[-2:]
        copies = []
        at = 0
        for n, piece in enumerate(pieces):
            copies.append(
                pltpu.make_async_copy(refs[n], out_ref.at[pl.ds(at, piece.shape[0])], sem.at[n])
            )
            at += piece.shape[0]
        for copy in copies:
            copy.start()
        for copy in copies:
            copy.wait()

    return run(
        body, [(p, ANY) for p in pieces] + [(tok, ANY)], [((count, rows, TB), pieces[0].dtype, ANY)], [DMA((len(pieces),))]
    )


def prepare(rows, low, high, ids, tok):
    def body(ids_ref, low_ref, high_ref, _, top_ref, rest_ref, pool, sem):
        one = pltpu.make_async_copy(low_ref, pool.at[pl.ds(0, HALF)], sem.at[0])
        two = pltpu.make_async_copy(high_ref, pool.at[pl.ds(HALF, HALF)], sem.at[1])
        one.start()
        two.start()
        mask = ids_ref[4]
        one.wait()
        two.wait()
        for i in range(KR):

            def step(j, c):
                at = pl.ds(pl.multiple_of(j * TB, TB), TB)
                h, lo = split2(pool[jnp.bitwise_xor(i * KC + j, mask)])
                top_ref[i * rows:(i + 1) * rows, at] = h
                rest_ref[i * rows:(i + 1) * rows, at] = lo
                return c

            lax.fori_loop(0, KC, step, 0, unroll=4)

    return run(
        body,
        [(ids, SMEM), (low, ANY), (high, ANY), (tok, ANY)],
        [((KR * rows, KC * TB), BF16, VMEM)] * 2,
        [pltpu.VMEM((K, rows, TB), F32), DMA((2,))],
    )


def arrange(inverse, tok):
    def body(inv_ref, _, top_ref, rest_ref):
        pieces = [inv_ref[:, i * TB + row:i * TB + row + n] for row, n in PARTS for i in range(KR)]
        top_ref[...], rest_ref[...] = split2(jnp.concatenate(pieces, axis=1))

    return run(body, [(inverse, VMEM), (tok, ANY)], [((PW, PW), BF16, VMEM)] * 2, [])


def update(groups, cols, sent, fronts, ids, inverse, pivots, out, tok):
    width = 512
    chunks = [(top + n * rows, rows) for top, rows, count in groups for n in range(count)]
    first = chunks[0][0]
    tall = sum(rows for _, rows in chunks)
    m = KR * tall
    at_pivots = 4 + 2 * len(groups)
    at_fronts = at_pivots + len(pivots)

    def body(ids_ref, inv_ref, low_ref, *refs):
        out_ref, left = refs[-2:]
        refs = (ids_ref, inv_ref, low_ref, None) + refs

        @pl.when(pl.program_id(0) == 0)
        def _():
            at = 0
            for n, (_, rows, count) in enumerate(groups):
                size = KR * rows * count
                own, other = refs[4 + 2 * n], refs[5 + 2 * n]
                h, lo = split2(jnp.where(ids_ref[2] == 0, own[...], other[...]).reshape(size, PW))
                both = jnp.dot(jnp.concatenate([h, lo], axis=0), inv_ref[...], preferred_element_type=F32)
                total = both[:size] + both[size:] + jnp.dot(h, low_ref[...], preferred_element_type=F32)
                left[at:at + size, :], left[m + at:m + at + size, :] = split2(total)
                at += size

        at, total = 0, 0.0
        for n, (_, size) in enumerate(PARTS):
            h = left[:, at:at + KR * size]
            both = jnp.dot(h, refs[at_pivots + 2 * n][...], preferred_element_type=F32)
            total += both[:m] + both[m:] + jnp.dot(h[:m], refs[at_pivots + 2 * n + 1][...], preferred_element_type=F32)
            at += KR * size
        at = 0
        for n, (row, rows) in enumerate(chunks):
            one = total[at:at + KR * rows].reshape(KR, rows, width)
            out_ref[:, row - first:row - first + rows, :] = refs[at_fronts + n][...] - one
            at += KR * rows

    square = pl.BlockSpec((PW, PW), lambda n: (0, 0))
    ins = [(ids, SMEM), (inverse[0], square), (inverse[1], square)]
    for (_, rows, count), own, other in zip(groups, cols, sent):
        pivot = pl.BlockSpec((count, KR, rows, PW), lambda n: (0, 0, 0, 0))
        ins += [(own, pivot), (other, pivot)]
    ins += [(p, pl.BlockSpec((p.shape[0], width), lambda n: (0, n))) for p in pivots]
    ins += [(f, pl.BlockSpec((KR, f.shape[1], width), lambda n: (0, 0, n))) for f in fronts]
    ins.append((tok, ANY))
    more = {}
    if out is not None:
        ins.append((out, ANY))
        more["input_output_aliases"] = {len(ins) - 1: 0}
    return run(
        body,
        ins,
        [((KR, TB, KC * TB), F32, pl.BlockSpec((KR, tall, width), lambda n: (0, first // tall, n)))],
        [pltpu.VMEM((2 * m, PW), BF16)],
        limit=24,
        grid=(KC * TB // width,),
        **more,
    )


class Plan:
    def __init__(self):
        self.steps, self.kernels = [], []

    def kernel(self, name, need, give, cost, call):
        self.kernels.append(name)
        self.steps.append((name, "kernel", need, give, cost, call))

    def permute(self, name, need, give, links, cost, call):
        self.steps.append((name, "permute", [need], [give], (links, cost), call))

    def emit(self):
        steps = {s[0]: s for s in self.steps}
        for number in ORDER:
            step = steps[self.kernels[number]]
            yield number, step
            for s in self.steps:
                if s[1] == "permute" and s[2][0] in step[3]:
                    yield None, s


def text(*parts):
    return "".join(str(p) for p in parts)


def flip(axis, bits):
    return lambda v: lax.ppermute(v, axis, [(i, i ^ bits) for i in range(lax.axis_size(axis))])


def make_plan(tiles, split, first, second, ids, pivot_inverse):
    level_links = (("core",), ("xa",), ("xa", "xb"), ("y",))
    link_time = (3.5, 22.8, 22.8, 22.8)
    plan = Plan()
    kernel, permute = plan.kernel, plan.permute

    def level_steps(group, index):
        top, rows, count = group
        row = top + index * rows
        n, g = text("c", row), text("g", top)
        share = rows / 32
        kernel(text(n, "k0"), [], [text(n, "s0"), text(n, "h0")], 0.6 + 0.4 * share, lambda v, tok: first_split(row, rows, tiles, split, tok))
        for level in range(LEVELS):
            permute(text(n, "p", level), text(n, "s", level), text(n, "r", level), level_links[level], link_time[level] * share, flip("cube", 1 << level))
            need = [text(n, "r", level), text(n, "h", level)]
            if level < LEVELS - 1:
                kernel(
                    text(n, "k", level + 1),
                    need,
                    [text(n, "s", level + 1), text(n, "h", level + 1)],
                    0.8 + 0.9 * share,
                    lambda v, tok, level=level: next_level(
                        level, rows, v[text(n, "h", level)], v[text(n, "r", level)], split, first, second, tok
                    ),
                )
            else:
                kernel(
                    text(n, "k4"),
                    need + ([text(g, "cols", index - 1)] if index else []),
                    [text(g, "cols", index), text(n, "front")],
                    0.8 + 0.9 * share,
                    lambda v, tok: last_level(
                        index, count, rows, v[text(n, "h3")], v[text(n, "r3")], first, second, v.get(text(g, "cols", index - 1)), tok
                    ),
                )
        if index == count - 1:
            permute(
                text(g, "pc"), text(g, "cols", index), text(g, "sent"), ("y",), 5.7 * share * count,
                lambda v: lax.ppermute(v, "col", [(0, 1)]),
            )

    def part_steps(index, row, rows):
        n = text("q", index)
        m = rows / 128

        def add(name, terms, cuts, cost):
            kernel(
                text(n, name), [text(n, t) for t in terms], [text(n, name, i) for i in range(len(cuts))], cost,
                lambda v, tok: add_cut([v[text(n, t)] for t in terms], cuts, rows, tok),
            )

        def move(name, what, axis, bits, links, cost):
            permute(text(n, name), text(n, what), text(n, name), links, cost, flip(axis, bits))

        def join(name, pieces, cost):
            kernel(text(n, name), [text(n, p) for p in pieces], [text(n, name)], cost, lambda v, tok: lay([v[text(n, p)] for p in pieces], rows, tok))

        kernel(text(n, "t"), ["weight"], [text(n, "keep"), text(n, "send")], 2 + 6 * m, lambda v, tok: parts_of(row, rows, v["weight"], tiles, tok))
        move("core", "send", "cube", 1, ("core",), 7 * m)
        add("a", ["keep", "core"], (64,), 0.5 + 2 * m)
        permute(text(n, "zs"), text(n, "a0"), text(n, "zs"), ("gather",), 16 + 30 * m, lambda v: lax.psum_scatter(v, "row", tiled=True))
        add("b", ["zs"], (8, 8), 0.5 + m)
        move("y", "b1", "cube", 8, ("y",), 11.4 * m)
        add("c", ["b0", "y"], (8,), 0.5)
        move("xa", "c0", "cube", 2, ("xa",), 11.4 * m)
        add("d", ["c0", "xa"], (8,), 0.5)
        move("xb", "d0", "cube", 6, ("xb",), 11.4 * m)
        add("e", ["d0", "xb"], (8,), 0.5)
        move("gy", "e0", "cube", 8, ("y",), 11.4 * m)
        join("h", ["e0", "gy"], 1)
        permute(text(n, "gz"), text(n, "h"), text(n, "gz"), ("gather",), 16 + 30 * m, lambda v: lax.all_gather(v, "row", tiled=True))
        join("low", ["gz"], 1 + 2 * m)
        move("high", "low", "cube", 1, ("core",), 7 * m)
        kernel(text(n, "m"), [text(n, "low"), text(n, "high")], [text(n, "m0"), text(n, "m1")], 4, lambda v, tok: prepare(rows, v[text(n, "low")], v[text(n, "high")], ids, tok))

    level_steps(GROUPS[0], 0)
    kernel("l0", [], ["ls0"], 0.6, lambda v, tok: own_lists(split, first, second, tok))
    for n, bits in enumerate((2, 4, 8, 1)):
        permute(text("lp", n), text("ls", n), text("lr", n), level_links[(1, 2, 3, 0)[n]], 0.2, flip("cube", bits))
        if n < 3:
            kernel(text("l", n + 1), [text("ls", n), text("lr", n)], [text("ls", n + 1)], 0.5, lambda v, tok, n=n: lay([v[text("ls", n)], v[text("lr", n)]], 16, tok))
    kernel("weight", ["ls3", "lr3"], ["weight"], 1.5, lambda v, tok: weights(ids, v["ls3"], v["lr3"], tok))
    for group in GROUPS:
        for index in range(group[2]):
            if group is not GROUPS[0] or index:
                level_steps(group, index)
    for index, part in enumerate(PARTS):
        part_steps(index, *part)
    kernel("inv", [], ["inv0", "inv1"], 2, lambda v, tok: arrange(pivot_inverse, tok))
    pivots = [text("q", i, "m", j) for i in range(len(PARTS)) for j in range(2)]
    start = 0
    for at, number in enumerate(CALLS):
        groups = GROUPS[start:start + number]
        start += number
        cols = [text("g", top, "cols", count - 1) for top, rows, count in groups]
        sent = [text("g", top, "sent") for top, rows, count in groups]
        fronts = [text("c", top + n * rows, "front") for top, rows, count in groups for n in range(count)]
        kernel(
            text("u", at), fronts + cols + sent + pivots + ["inv0", "inv1"] + ([text("out", at - 1)] if at else []), [text("out", at)], 8,
            lambda v, tok, at=at, groups=groups, names=(cols, sent, fronts): update(
                groups, *[[v[n] for n in x] for x in names], ids, (v["inv0"], v["inv1"]), [v[p] for p in pivots], v.get(text("out", at - 1)), tok
            ),
        )

    return plan


def body(update_tiles, split_order, first_source, second_source, pivot_inverse):
    tiles = pltpu.with_memory_space_constraint(update_tiles.reshape(K, TB, TB), pltpu.HBM)
    split, first, second = (x.reshape(LEVELS, K) for x in (split_order, first_source, second_source))
    cube, row_at, col = lax.axis_index("cube"), lax.axis_index("row"), lax.axis_index("col")
    mask = (cube & 1) * 64 + row_at * 16 + (cube >> 3) * 8
    ids = jnp.stack([cube, row_at, col, mask, mask - row_at * 16]).astype(jnp.int32)
    plan = make_plan(tiles, split, first, second, ids, pivot_inverse)
    values = {}
    tok = ids
    for number, (name, kind, need, give, _, call) in plan.emit():
        if number is not None:
            FLOPS[0] = int(WORK.get(number, 0) * 2.2e10)
            with jax.named_scope(name):
                results = call(values, tok)
            tok = results[0]
            values.update(zip(give, results))
        else:
            with jax.named_scope(name):
                values[give[0]] = call(values[need[0]])
    return values[text("out", len(CALLS) - 1)].reshape(1, 1, 1, KR * TB, KC * TB)


def solution(mesh):
    return jax.shard_map(
        body,
        mesh=mesh,
        in_specs=(
            P("cube", "row", "col", None, None, None),
            P("cube", "row", "col", None, None),
            P("cube", "row", "col", None, None),
            P("cube", "row", "col", None, None),
            P(),
        ),
        out_specs=P("cube", "row", "col", None, None),
        check_vma=False,
    )
```

```python
import jax
import jax.numpy as jnp
from jax import lax
from jax.experimental import pallas as pl
from jax.experimental.pallas import tpu as pltpu
from jax.sharding import PartitionSpec as P

TB = 128
KR = 4
KC = 32
PW = 512
K = 128
HALF = 64
LEVELS = 4
F32 = jnp.float32
BF16 = jnp.bfloat16

GROUPS = ((0, 24, 4), (96, 16, 2))
CALLS = (1, 1)
ORDER = (
    10, 0, 5, 11, 6, 7, 1, 8, 9, 35, 44, 12, 15, 36, 20, 2, 25, 21, 45, 13, 37, 16, 30, 26, 3, 38, 53, 39, 46, 17,
    40, 47, 4, 41, 27, 48, 49, 22, 14, 50, 18, 23, 42, 31, 28, 19, 24, 32, 51, 52, 33, 43, 54, 29, 34, 55,
)
WORK = {
    0: 0.05, 1: 0.8, 2: 0.8, 3: 0.05, 6: 0.2, 7: 0.4, 8: 0.05, 9: 0.05, 10: 0.4, 11: 0.05, 12: 0.8, 13: 0.8, 14:
    0.8, 15: 0.8, 16: 0.05, 17: 0.05, 19: 0.8, 20: 0.8, 22: 0.8, 23: 0.2, 24: 0.4, 25: 0.8, 26: 0.4, 27: 0.05, 29:
    0.2, 30: 0.4, 34: 0.2, 36: 0.1, 37: 0.05, 38: 0.4, 39: 0.2, 46: 0.05, 48: 0.8, 49: 0.2, 50: 0.4, 51: 0.8,
}
PARTS = ((0, 64), (64, 64))

ANY = pl.BlockSpec(memory_space=pl.ANY)
HBM = pl.BlockSpec(memory_space=pltpu.HBM)
SMEM = pl.BlockSpec(memory_space=pltpu.SMEM)
VMEM = pl.BlockSpec(memory_space=pltpu.VMEM)
DMA = pltpu.SemaphoreType.DMA


def nt(a, b):
    return lax.dot_general(a, b, (((1,), (1,)), ((), ())), preferred_element_type=F32)


def split2(x):
    high = x.astype(BF16)
    return high, (x - high.astype(F32)).astype(BF16)


FLOPS = [0]


def run(body, ins, outs, scratch, limit=16, **more):
    return pl.pallas_call(
        body,
        in_specs=[ANY if s is HBM else s for _, s in ins],
        out_specs=[ANY if s is HBM else s for _, _, s in outs],
        out_shape=[pltpu.HBM(s, d) if spec is HBM else jax.ShapeDtypeStruct(s, d) for s, d, spec in outs],
        scratch_shapes=scratch,
        compiler_params=pltpu.CompilerParams(vmem_limit_bytes=limit << 20),
        cost_estimate=pl.CostEstimate(flops=FLOPS[0], bytes_accessed=0, transcendentals=0),
        **more,
    )(*[pltpu.with_memory_space_constraint(a, pltpu.HBM) if s is HBM else a for a, s in ins])


def first_split(row, rows, tiles, split, tok):
    def body(split_ref, tiles_ref, _, send_ref, keep_ref, pool, buf, sem):
        get = pltpu.make_async_copy(tiles_ref.at[:, pl.ds(row, rows), :], pool, sem.at[0])
        get.start()
        get.wait()

        def step(i, c):
            buf[i] = pool[split_ref[0, i]]
            return c

        lax.fori_loop(0, HALF, step, 0, unroll=8)
        one = pltpu.make_async_copy(buf.at[pl.ds(0, HALF)], send_ref, sem.at[1])
        one.start()
        lax.fori_loop(HALF, K, step, 0, unroll=8)
        two = pltpu.make_async_copy(buf.at[pl.ds(HALF, HALF)], keep_ref, sem.at[2])
        two.start()
        one.wait()
        two.wait()

    return run(
        body,
        [(split, SMEM), (tiles, ANY), (tok, ANY)],
        [((HALF, rows, TB), F32, ANY), ((HALF, rows, TB), F32, HBM)],
        [pltpu.VMEM((K, rows, TB), F32), pltpu.VMEM((K, rows, TB), F32), DMA((3,))],
    )


def fetch(kept_ref, recv_ref, pool, sem):
    one = pltpu.make_async_copy(kept_ref, pool.at[pl.ds(0, HALF)], sem.at[0])
    two = pltpu.make_async_copy(recv_ref, pool.at[pl.ds(HALF, HALF)], sem.at[1])
    one.start()
    two.start()
    one.wait()
    two.wait()


def next_level(level, rows, kept, recv, split, first, second, tok):
    def body(split_ref, first_ref, second_ref, kept_ref, recv_ref, _, send_ref, keep_ref, pool, buf, sem):
        fetch(kept_ref, recv_ref, pool, sem)

        def step(i, c):
            t = split_ref[level + 1, i]
            buf[i] = pool[first_ref[level, t]] + pool[second_ref[level, t]]
            return c

        lax.fori_loop(0, HALF, step, 0, unroll=8)
        one = pltpu.make_async_copy(buf.at[pl.ds(0, HALF)], send_ref, sem.at[2])
        one.start()
        lax.fori_loop(HALF, K, step, 0, unroll=8)
        two = pltpu.make_async_copy(buf.at[pl.ds(HALF, HALF)], keep_ref, sem.at[3])
        two.start()
        one.wait()
        two.wait()

    return run(
        body,
        [(split, SMEM), (first, SMEM), (second, SMEM), (kept, HBM), (recv, ANY), (tok, ANY)],
        [((HALF, rows, TB), F32, ANY), ((HALF, rows, TB), F32, HBM)],
        [pltpu.VMEM((K, rows, TB), F32), pltpu.VMEM((K, rows, TB), F32), DMA((4,))],
    )


def last_level(index, count, rows, kept, recv, first, second, before, tok):
    def body(first_ref, second_ref, kept_ref, recv_ref, *refs):
        cols_ref, front_ref, pool, buf, cbuf, sem = refs[-6:]
        level = LEVELS - 1
        fetch(kept_ref, recv_ref, pool, sem)
        for i in range(KR):
            for j in range(PW // TB):
                t = i * KC + j
                tile = pool[first_ref[level, t]] + pool[second_ref[level, t]]
                buf[i, :, j * TB:(j + 1) * TB] = tile
                cbuf[i, :, j * TB:(j + 1) * TB] = tile
        one = pltpu.make_async_copy(cbuf, cols_ref.at[index], sem.at[2])
        one.start()
        for i in range(KR):

            def step(j, c):
                t = i * KC + j
                at = pl.ds(pl.multiple_of(j * TB, TB), TB)
                buf[i, :, at] = pool[first_ref[level, t]] + pool[second_ref[level, t]]
                return c

            lax.fori_loop(PW // TB, KC, step, 0, unroll=4)
        two = pltpu.make_async_copy(buf, front_ref, sem.at[3])
        two.start()
        one.wait()
        two.wait()

    ins = [(first, SMEM), (second, SMEM), (kept, HBM), (recv, ANY), (tok, ANY)]
    more = {}
    if before is not None:
        ins.append((before, ANY))
        more["input_output_aliases"] = {len(ins) - 1: 0}
    return run(
        body,
        ins,
        [((count, KR, rows, PW), F32, ANY), ((KR, rows, KC * TB), F32, HBM)],
        [
            pltpu.VMEM((K, rows, TB), F32),
            pltpu.VMEM((KR, rows, KC * TB), F32),
            pltpu.VMEM((KR, rows, PW), F32),
            DMA((4,)),
        ],
        **more,
    )


def flips(bits):
    return ((bits >> 1) & 1) + ((bits >> 2) & 1) * 2 + ((bits >> 3) & 1) * 4 + (bits & 1) * 8


def own_lists(split, first, second, tok):
    def body(split_ref, first_ref, second_ref, _, out_ref):
        out_ref[0, 0:4, :] = split_ref[...]
        out_ref[0, 4:8, :] = first_ref[...]
        out_ref[0, 8:12, :] = second_ref[...]
        order = split_ref[...]
        out_ref[0, 12:16, :] = jnp.concatenate([order[:, HALF:], order[:, :HALF]], axis=1)

    return run(body, [(split, VMEM), (first, VMEM), (second, VMEM), (tok, ANY)], [((1, 16, K), jnp.int32, VMEM)], [])


def weights(ids, near, far, tok):
    def body(ids_ref, near_ref, far_ref, _, out_ref, lists_ref):
        lists_ref[0:8] = near_ref[...]
        lists_ref[8:16] = far_ref[...]
        cube = ids_ref[0]
        row = lax.broadcasted_iota(jnp.int32, (K, K), 0)
        lane = lax.broadcasted_iota(jnp.int32, (K, K), 1)
        mine = jnp.logical_and(lane == jnp.bitwise_xor(row, ids_ref[3]), ids_ref[1] == 0)
        weight = jnp.where(mine, 1.0, 0.0).astype(BF16)
        for level in range(LEVELS - 1, -1, -1):
            parent = lists_ref[flips(cube & ((2 << level) - 1))]
            child = lists_ref[flips(cube & ((1 << level) - 1))]
            one = jnp.where(row == parent[4 + level:5 + level, :], 1.0, 0.0)
            two = jnp.where(row == parent[8 + level:9 + level, :], 1.0, 0.0)
            joined = nt(weight, (one + two).astype(BF16))
            bit = (cube >> level) & 1
            joined = jnp.where((lane >> 6) == bit, joined, 0.0).astype(BF16)
            order = jnp.where(row == child[12 + level:13 + level, :], 1.0, 0.0).astype(BF16)
            weight = nt(joined, order).astype(BF16)
        out_ref[...] = weight.astype(F32)

    return run(
        body,
        [(ids, SMEM), (near, VMEM), (far, VMEM), (tok, ANY)],
        [((K, K), F32, VMEM)],
        [pltpu.VMEM((16, 16, K), jnp.int32)],
    )


def parts_of(row, rows, weight, tiles, tok):
    def body(weight_ref, tiles_ref, _, keep_ref, send_ref, pool, buf, sem):
        get = pltpu.make_async_copy(tiles_ref.at[:, pl.ds(row, rows), :], pool, sem.at[0])
        get.start()
        w = weight_ref[...].astype(BF16)
        w = jnp.concatenate([w, w], axis=1)
        get.wait()
        flat = pool.reshape(K * rows, TB)
        out = buf.reshape(K * rows, TB)

        def step(n, carry):
            at = n * 2
            x = jnp.concatenate(
                [flat[pl.ds(at, K, stride=rows), :], flat[pl.ds(at + 1, K, stride=rows), :]], axis=1
            )
            y = jnp.dot(w, jnp.concatenate(split2(x), axis=0), preferred_element_type=F32)
            out[pl.ds(at, K, stride=rows), :] = y[:, :TB]
            out[pl.ds(at + 1, K, stride=rows), :] = y[:, TB:]
            return carry

        lax.fori_loop(0, rows // 2, step, 0, unroll=4)
        one = pltpu.make_async_copy(buf.at[pl.ds(0, HALF)], keep_ref, sem.at[1])
        two = pltpu.make_async_copy(buf.at[pl.ds(HALF, HALF)], send_ref, sem.at[2])
        one.start()
        two.start()
        one.wait()
        two.wait()

    return run(
        body,
        [(weight, VMEM), (tiles, ANY), (tok, ANY)],
        [((HALF, rows, TB), F32, ANY)] * 2,
        [pltpu.VMEM((K, rows, TB), F32), pltpu.VMEM((K, rows, TB), F32), DMA((3,))],
    )


def add_cut(terms, cuts, rows, tok):
    def body(*refs):
        total = refs[0][...]
        for term in refs[1:len(terms)]:
            total = total + term[...]
        at = 0
        for cut, ref in zip(cuts, refs[len(terms) + 1:]):
            ref[...] = total[at:at + cut]
            at += cut

    return run(
        body, [(t, VMEM) for t in terms] + [(tok, ANY)], [((cut, rows, TB), F32, VMEM) for cut in cuts], []
    )


def lay(pieces, rows, tok):
    count = sum(p.shape[0] for p in pieces)

    def body(*refs):
        out_ref, sem = refs[-2:]
        copies = []
        at = 0
        for n, piece in enumerate(pieces):
            copies.append(
                pltpu.make_async_copy(refs[n], out_ref.at[pl.ds(at, piece.shape[0])], sem.at[n])
            )
            at += piece.shape[0]
        for copy in copies:
            copy.start()
        for copy in copies:
            copy.wait()

    return run(
        body, [(p, ANY) for p in pieces] + [(tok, ANY)], [((count, rows, TB), pieces[0].dtype, ANY)], [DMA((len(pieces),))]
    )


def prepare(rows, low, high, ids, tok):
    def body(ids_ref, low_ref, high_ref, _, top_ref, rest_ref, pool, sem):
        one = pltpu.make_async_copy(low_ref, pool.at[pl.ds(0, HALF)], sem.at[0])
        two = pltpu.make_async_copy(high_ref, pool.at[pl.ds(HALF, HALF)], sem.at[1])
        one.start()
        two.start()
        mask = ids_ref[4]
        one.wait()
        two.wait()
        for i in range(KR):

            def step(j, c):
                at = pl.ds(pl.multiple_of(j * TB, TB), TB)
                h, lo = split2(pool[jnp.bitwise_xor(i * KC + j, mask)])
                top_ref[i * rows:(i + 1) * rows, at] = h
                rest_ref[i * rows:(i + 1) * rows, at] = lo
                return c

            lax.fori_loop(0, KC, step, 0, unroll=4)

    return run(
        body,
        [(ids, SMEM), (low, ANY), (high, ANY), (tok, ANY)],
        [((KR * rows, KC * TB), BF16, VMEM)] * 2,
        [pltpu.VMEM((K, rows, TB), F32), DMA((2,))],
    )


def arrange(inverse, tok):
    def body(inv_ref, _, top_ref, rest_ref):
        pieces = [inv_ref[:, i * TB + row:i * TB + row + n] for row, n in PARTS for i in range(KR)]
        top_ref[...], rest_ref[...] = split2(jnp.concatenate(pieces, axis=1))

    return run(body, [(inverse, VMEM), (tok, ANY)], [((PW, PW), BF16, VMEM)] * 2, [])


def update(groups, cols, sent, fronts, ids, inverse, pivots, out, tok):
    width = 512
    chunks = [(top + n * rows, rows) for top, rows, count in groups for n in range(count)]
    first = chunks[0][0]
    tall = sum(rows for _, rows in chunks)
    m = KR * tall
    at_pivots = 4 + 2 * len(groups)
    at_fronts = at_pivots + len(pivots)

    def body(ids_ref, inv_ref, low_ref, *refs):
        out_ref, end_ref, left = refs[-3:]
        refs = (ids_ref, inv_ref, low_ref, None) + refs
        end_ref[...] = jnp.zeros_like(end_ref)

        @pl.when(pl.program_id(0) == 0)
        def _():
            at = 0
            for n, (_, rows, count) in enumerate(groups):
                size = KR * rows * count
                own, other = refs[4 + 2 * n], refs[5 + 2 * n]
                h, lo = split2(jnp.where(ids_ref[2] == 0, own[...], other[...]).reshape(size, PW))
                both = jnp.dot(jnp.concatenate([h, lo], axis=0), inv_ref[...], preferred_element_type=F32)
                total = both[:size] + both[size:] + jnp.dot(h, low_ref[...], preferred_element_type=F32)
                left[at:at + size, :], left[m + at:m + at + size, :] = split2(total)
                at += size

        at, total = 0, 0.0
        for n, (_, size) in enumerate(PARTS):
            h = left[:, at:at + KR * size]
            both = jnp.dot(h, refs[at_pivots + 2 * n][...], preferred_element_type=F32)
            total += both[:m] + both[m:] + jnp.dot(h[:m], refs[at_pivots + 2 * n + 1][...], preferred_element_type=F32)
            at += KR * size
        at = 0
        for n, (row, rows) in enumerate(chunks):
            one = total[at:at + KR * rows].reshape(KR, rows, width)
            out_ref[:, row - first:row - first + rows, :] = refs[at_fronts + n][...] - one
            at += KR * rows

    square = pl.BlockSpec((PW, PW), lambda n: (0, 0))
    ins = [(ids, SMEM), (inverse[0], square), (inverse[1], square)]
    for (_, rows, count), own, other in zip(groups, cols, sent):
        pivot = pl.BlockSpec((count, KR, rows, PW), lambda n: (0, 0, 0, 0))
        ins += [(own, pivot), (other, pivot)]
    ins += [(p, pl.BlockSpec((p.shape[0], width), lambda n: (0, n))) for p in pivots]
    ins += [(f, pl.BlockSpec((KR, f.shape[1], width), lambda n: (0, 0, n))) for f in fronts]
    ins.append((tok, ANY))
    more = {}
    if out is not None:
        ins.append((out, ANY))
        more["input_output_aliases"] = {len(ins) - 1: 0}
    return run(
        body,
        ins,
        [
            ((KR, TB, KC * TB), F32, pl.BlockSpec((KR, tall, width), lambda n: (0, first // tall, n))),
            ((8, TB), F32, pl.BlockSpec((8, TB), lambda n: (0, 0))),
        ],
        [pltpu.VMEM((2 * m, PW), BF16)],
        limit=24,
        grid=(KC * TB // width,),
        **more,
    )


class Plan:
    def __init__(self):
        self.steps, self.kernels = [], []

    def kernel(self, name, need, give, cost, call):
        self.kernels.append(name)
        self.steps.append((name, "kernel", need, give, cost, call))

    def permute(self, name, need, give, links, cost, call):
        self.steps.append((name, "permute", [need], [give], (links, cost), call))

    def emit(self):
        steps = {s[0]: s for s in self.steps}
        for number in ORDER:
            step = steps[self.kernels[number]]
            yield number, step
            for s in self.steps:
                if s[1] == "permute" and s[2][0] in step[3]:
                    yield None, s


def text(*parts):
    return "".join(str(p) for p in parts)


def flip(axis, bits):
    return lambda v: lax.ppermute(v, axis, [(i, i ^ bits) for i in range(lax.axis_size(axis))])


def make_plan(tiles, split, first, second, ids, pivot_inverse):
    level_links = (("core",), ("xa",), ("xa", "xb"), ("y",))
    link_time = (3.5, 22.8, 22.8, 22.8)
    plan = Plan()
    kernel, permute = plan.kernel, plan.permute

    def level_steps(group, index):
        top, rows, count = group
        row = top + index * rows
        n, g = text("c", row), text("g", top)
        share = rows / 32
        kernel(text(n, "k0"), [], [text(n, "s0"), text(n, "h0")], 0.6 + 0.4 * share, lambda v, tok: first_split(row, rows, tiles, split, tok))
        for level in range(LEVELS):
            permute(text(n, "p", level), text(n, "s", level), text(n, "r", level), level_links[level], link_time[level] * share, flip("cube", 1 << level))
            need = [text(n, "r", level), text(n, "h", level)]
            if level < LEVELS - 1:
                kernel(
                    text(n, "k", level + 1),
                    need,
                    [text(n, "s", level + 1), text(n, "h", level + 1)],
                    0.8 + 0.9 * share,
                    lambda v, tok, level=level: next_level(
                        level, rows, v[text(n, "h", level)], v[text(n, "r", level)], split, first, second, tok
                    ),
                )
            else:
                kernel(
                    text(n, "k4"),
                    need + ([text(g, "cols", index - 1)] if index else []),
                    [text(g, "cols", index), text(n, "front")],
                    0.8 + 0.9 * share,
                    lambda v, tok: last_level(
                        index, count, rows, v[text(n, "h3")], v[text(n, "r3")], first, second, v.get(text(g, "cols", index - 1)), tok
                    ),
                )
        if index == count - 1:
            permute(
                text(g, "pc"), text(g, "cols", index), text(g, "sent"), ("y",), 5.7 * share * count,
                lambda v: lax.ppermute(v, "col", [(0, 1)]),
            )

    def part_steps(index, row, rows):
        n = text("q", index)
        m = rows / 128

        def add(name, terms, cuts, cost):
            kernel(
                text(n, name), [text(n, t) for t in terms], [text(n, name, i) for i in range(len(cuts))], cost,
                lambda v, tok: add_cut([v[text(n, t)] for t in terms], cuts, rows, tok),
            )

        def move(name, what, axis, bits, links, cost):
            permute(text(n, name), text(n, what), text(n, name), links, cost, flip(axis, bits))

        def join(name, pieces, cost):
            kernel(text(n, name), [text(n, p) for p in pieces], [text(n, name)], cost, lambda v, tok: lay([v[text(n, p)] for p in pieces], rows, tok))

        kernel(text(n, "t"), ["weight"], [text(n, "keep"), text(n, "send")], 2 + 6 * m, lambda v, tok: parts_of(row, rows, v["weight"], tiles, tok))
        move("core", "send", "cube", 1, ("core",), 7 * m)
        add("a", ["keep", "core"], (64,), 0.5 + 2 * m)
        permute(text(n, "zs"), text(n, "a0"), text(n, "zs"), ("gather",), 16 + 30 * m, lambda v: lax.psum_scatter(v, "row", tiled=True))
        add("b", ["zs"], (8, 8), 0.5 + m)
        move("y", "b1", "cube", 8, ("y",), 11.4 * m)
        add("c", ["b0", "y"], (8,), 0.5)
        move("xa", "c0", "cube", 2, ("xa",), 11.4 * m)
        add("d", ["c0", "xa"], (8,), 0.5)
        move("xb", "d0", "cube", 6, ("xb",), 11.4 * m)
        add("e", ["d0", "xb"], (8,), 0.5)
        move("gy", "e0", "cube", 8, ("y",), 11.4 * m)
        join("h", ["e0", "gy"], 1)
        permute(text(n, "gz"), text(n, "h"), text(n, "gz"), ("gather",), 16 + 30 * m, lambda v: lax.all_gather(v, "row", tiled=True))
        join("low", ["gz"], 1 + 2 * m)
        move("high", "low", "cube", 1, ("core",), 7 * m)
        kernel(text(n, "m"), [text(n, "low"), text(n, "high")], [text(n, "m0"), text(n, "m1")], 4, lambda v, tok: prepare(rows, v[text(n, "low")], v[text(n, "high")], ids, tok))

    level_steps(GROUPS[0], 0)
    kernel("l0", [], ["ls0"], 0.6, lambda v, tok: own_lists(split, first, second, tok))
    for n, bits in enumerate((2, 4, 8, 1)):
        permute(text("lp", n), text("ls", n), text("lr", n), level_links[(1, 2, 3, 0)[n]], 0.2, flip("cube", bits))
        if n < 3:
            kernel(text("l", n + 1), [text("ls", n), text("lr", n)], [text("ls", n + 1)], 0.5, lambda v, tok, n=n: lay([v[text("ls", n)], v[text("lr", n)]], 16, tok))
    kernel("weight", ["ls3", "lr3"], ["weight"], 1.5, lambda v, tok: weights(ids, v["ls3"], v["lr3"], tok))
    for group in GROUPS:
        for index in range(group[2]):
            if group is not GROUPS[0] or index:
                level_steps(group, index)
    for index, part in enumerate(PARTS):
        part_steps(index, *part)
    kernel("inv", [], ["inv0", "inv1"], 2, lambda v, tok: arrange(pivot_inverse, tok))
    pivots = [text("q", i, "m", j) for i in range(len(PARTS)) for j in range(2)]
    start = 0
    for at, number in enumerate(CALLS):
        groups = GROUPS[start:start + number]
        start += number
        cols = [text("g", top, "cols", count - 1) for top, rows, count in groups]
        sent = [text("g", top, "sent") for top, rows, count in groups]
        fronts = [text("c", top + n * rows, "front") for top, rows, count in groups for n in range(count)]
        kernel(
            text("u", at), fronts + cols + sent + pivots + ["inv0", "inv1"] + ([text("out", at - 1)] if at else []), [text("out", at)], 8,
            lambda v, tok, at=at, groups=groups, names=(cols, sent, fronts): update(
                groups, *[[v[n] for n in x] for x in names], ids, (v["inv0"], v["inv1"]), [v[p] for p in pivots], v.get(text("out", at - 1)), tok
            ),
        )

    return plan


def body(update_tiles, split_order, first_source, second_source, pivot_inverse):
    tiles = pltpu.with_memory_space_constraint(update_tiles.reshape(K, TB, TB), pltpu.HBM)
    split, first, second = (x.reshape(LEVELS, K) for x in (split_order, first_source, second_source))
    cube, row_at, col = lax.axis_index("cube"), lax.axis_index("row"), lax.axis_index("col")
    mask = (cube & 1) * 64 + row_at * 16 + (cube >> 3) * 8
    ids = jnp.stack([cube, row_at, col, mask, mask - row_at * 16]).astype(jnp.int32)
    plan = make_plan(tiles, split, first, second, ids, pivot_inverse)
    values = {}
    tok = ids
    for number, (name, kind, need, give, _, call) in plan.emit():
        if number is not None:
            FLOPS[0] = int(WORK.get(number, 0) * 2.2e10)
            with jax.named_scope(name):
                results = call(values, tok)
            tok = results[1] if give[0].startswith("out") else results[0]
            values.update(zip(give, results))
        else:
            with jax.named_scope(name):
                values[give[0]] = call(values[need[0]])
    return values[text("out", len(CALLS) - 1)].reshape(1, 1, 1, KR * TB, KC * TB)


def solution(mesh):
    return jax.shard_map(
        body,
        mesh=mesh,
        in_specs=(
            P("cube", "row", "col", None, None, None),
            P("cube", "row", "col", None, None),
            P("cube", "row", "col", None, None),
            P("cube", "row", "col", None, None),
            P(),
        ),
        out_specs=P("cube", "row", "col", None, None),
        check_vma=False,
    )
```

```python
import jax
import jax.numpy as jnp
from jax import lax
from jax.experimental import pallas as pl
from jax.experimental.pallas import tpu as pltpu
from jax.sharding import PartitionSpec as P

TB = 128
KR = 4
KC = 32
PW = 512
K = 128
HALF = 64
LEVELS = 4
F32 = jnp.float32
BF16 = jnp.bfloat16

GROUPS = ((0, 24, 4), (96, 16, 2))
CALLS = (1, 1)
ORDER = (
    10, 0, 5, 11, 6, 7, 1, 8, 9, 35, 44, 12, 15, 36, 20, 2, 25, 21, 45, 13, 37, 16, 30, 26, 3, 38, 53, 39, 46, 17,
    40, 47, 4, 41, 27, 48, 49, 22, 14, 50, 18, 23, 42, 31, 28, 19, 24, 32, 51, 52, 33, 43, 54, 29, 34, 55,
)
WORK = {
    0: 0.05, 1: 0.8, 2: 0.8, 3: 0.05, 6: 0.2, 7: 0.4, 8: 0.05, 9: 0.05, 10: 0.4, 11: 0.05, 12: 0.8, 13: 0.8, 14:
    0.8, 15: 0.8, 16: 0.05, 17: 0.05, 19: 0.8, 20: 0.8, 22: 0.8, 23: 0.2, 24: 0.4, 25: 0.8, 26: 0.4, 27: 0.05, 29:
    0.2, 30: 0.4, 34: 0.2, 36: 0.1, 37: 0.05, 38: 0.4, 39: 0.2, 46: 0.05, 48: 0.8, 49: 0.2, 50: 0.4, 51: 0.8,
}
PARTS = ((0, 64), (64, 64))

ANY = pl.BlockSpec(memory_space=pl.ANY)
HBM = pl.BlockSpec(memory_space=pltpu.HBM)
SMEM = pl.BlockSpec(memory_space=pltpu.SMEM)
VMEM = pl.BlockSpec(memory_space=pltpu.VMEM)
DMA = pltpu.SemaphoreType.DMA


def nt(a, b):
    return lax.dot_general(a, b, (((1,), (1,)), ((), ())), preferred_element_type=F32)


def split2(x):
    high = x.astype(BF16)
    return high, (x - high.astype(F32)).astype(BF16)


FLOPS = [0]


def run(body, ins, outs, scratch, limit=32, **more):
    return pl.pallas_call(
        body,
        in_specs=[ANY if s is HBM else s for _, s in ins],
        out_specs=[ANY if s is HBM else s for _, _, s in outs],
        out_shape=[pltpu.HBM(s, d) if spec is HBM else jax.ShapeDtypeStruct(s, d) for s, d, spec in outs],
        scratch_shapes=scratch,
        compiler_params=pltpu.CompilerParams(vmem_limit_bytes=limit << 20),
        cost_estimate=pl.CostEstimate(flops=FLOPS[0], bytes_accessed=0, transcendentals=0),
        **more,
    )(*[pltpu.with_memory_space_constraint(a, pltpu.HBM) if s is HBM else a for a, s in ins])


def first_split(row, rows, tiles, split, tok):
    def body(split_ref, tiles_ref, _, send_ref, keep_ref, pool, buf, sem):
        get = pltpu.make_async_copy(tiles_ref.at[:, pl.ds(row, rows), :], pool, sem.at[0])
        get.start()
        get.wait()

        def step(i, c):
            buf[i] = pool[split_ref[0, i]]
            return c

        lax.fori_loop(0, HALF, step, 0, unroll=8)
        one = pltpu.make_async_copy(buf.at[pl.ds(0, HALF)], send_ref, sem.at[1])
        one.start()
        lax.fori_loop(HALF, K, step, 0, unroll=8)
        two = pltpu.make_async_copy(buf.at[pl.ds(HALF, HALF)], keep_ref, sem.at[2])
        two.start()
        one.wait()
        two.wait()

    return run(
        body,
        [(split, SMEM), (tiles, ANY), (tok, ANY)],
        [((HALF, rows, TB), F32, ANY)] * 2,
        [pltpu.VMEM((K, rows, TB), F32), pltpu.VMEM((K, rows, TB), F32), DMA((3,))],
    )


def fetch(kept_ref, recv_ref, pool, sem):
    one = pltpu.make_async_copy(kept_ref, pool.at[pl.ds(0, HALF)], sem.at[0])
    two = pltpu.make_async_copy(recv_ref, pool.at[pl.ds(HALF, HALF)], sem.at[1])
    one.start()
    two.start()
    one.wait()
    two.wait()


def next_level(level, rows, kept, recv, split, first, second, tok):
    def body(split_ref, first_ref, second_ref, kept_ref, recv_ref, _, send_ref, keep_ref, pool, buf, sem):
        fetch(kept_ref, recv_ref, pool, sem)

        def step(i, c):
            t = split_ref[level + 1, i]
            buf[i] = pool[first_ref[level, t]] + pool[second_ref[level, t]]
            return c

        lax.fori_loop(0, HALF, step, 0, unroll=8)
        one = pltpu.make_async_copy(buf.at[pl.ds(0, HALF)], send_ref, sem.at[2])
        one.start()
        lax.fori_loop(HALF, K, step, 0, unroll=8)
        two = pltpu.make_async_copy(buf.at[pl.ds(HALF, HALF)], keep_ref, sem.at[3])
        two.start()
        one.wait()
        two.wait()

    return run(
        body,
        [(split, SMEM), (first, SMEM), (second, SMEM), (kept, ANY), (recv, ANY), (tok, ANY)],
        [((HALF, rows, TB), F32, ANY)] * 2,
        [pltpu.VMEM((K, rows, TB), F32), pltpu.VMEM((K, rows, TB), F32), DMA((4,))],
    )


def last_level(index, count, rows, kept, recv, first, second, before, tok):
    def body(first_ref, second_ref, kept_ref, recv_ref, *refs):
        cols_ref, front_ref, pool, buf, cbuf, sem = refs[-6:]
        level = LEVELS - 1
        fetch(kept_ref, recv_ref, pool, sem)
        for i in range(KR):
            for j in range(PW // TB):
                t = i * KC + j
                tile = pool[first_ref[level, t]] + pool[second_ref[level, t]]
                buf[i, :, j * TB:(j + 1) * TB] = tile
                cbuf[i, :, j * TB:(j + 1) * TB] = tile
        one = pltpu.make_async_copy(cbuf, cols_ref.at[index], sem.at[2])
        one.start()
        for i in range(KR):

            def step(j, c):
                t = i * KC + j
                at = pl.ds(pl.multiple_of(j * TB, TB), TB)
                buf[i, :, at] = pool[first_ref[level, t]] + pool[second_ref[level, t]]
                return c

            lax.fori_loop(PW // TB, KC, step, 0, unroll=4)
        two = pltpu.make_async_copy(buf, front_ref, sem.at[3])
        two.start()
        one.wait()
        two.wait()

    ins = [(first, SMEM), (second, SMEM), (kept, ANY), (recv, ANY), (tok, ANY)]
    more = {}
    if before is not None:
        ins.append((before, ANY))
        more["input_output_aliases"] = {len(ins) - 1: 0}
    return run(
        body,
        ins,
        [((count, KR, rows, PW), F32, ANY), ((KR, rows, KC * TB), F32, HBM)],
        [
            pltpu.VMEM((K, rows, TB), F32),
            pltpu.VMEM((KR, rows, KC * TB), F32),
            pltpu.VMEM((KR, rows, PW), F32),
            DMA((4,)),
        ],
        **more,
    )


def flips(bits):
    return ((bits >> 1) & 1) + ((bits >> 2) & 1) * 2 + ((bits >> 3) & 1) * 4 + (bits & 1) * 8


def own_lists(split, first, second, tok):
    def body(split_ref, first_ref, second_ref, _, out_ref):
        out_ref[0, 0:4, :] = split_ref[...]
        out_ref[0, 4:8, :] = first_ref[...]
        out_ref[0, 8:12, :] = second_ref[...]
        order = split_ref[...]
        out_ref[0, 12:16, :] = jnp.concatenate([order[:, HALF:], order[:, :HALF]], axis=1)

    return run(body, [(split, VMEM), (first, VMEM), (second, VMEM), (tok, ANY)], [((1, 16, K), jnp.int32, VMEM)], [])


def weights(ids, near, far, tok):
    def body(ids_ref, near_ref, far_ref, _, out_ref, lists_ref):
        lists_ref[0:8] = near_ref[...]
        lists_ref[8:16] = far_ref[...]
        cube = ids_ref[0]
        row = lax.broadcasted_iota(jnp.int32, (K, K), 0)
        lane = lax.broadcasted_iota(jnp.int32, (K, K), 1)
        mine = jnp.logical_and(lane == jnp.bitwise_xor(row, ids_ref[3]), ids_ref[1] == 0)
        weight = jnp.where(mine, 1.0, 0.0).astype(BF16)
        for level in range(LEVELS - 1, -1, -1):
            parent = lists_ref[flips(cube & ((2 << level) - 1))]
            child = lists_ref[flips(cube & ((1 << level) - 1))]
            one = jnp.where(row == parent[4 + level:5 + level, :], 1.0, 0.0)
            two = jnp.where(row == parent[8 + level:9 + level, :], 1.0, 0.0)
            joined = nt(weight, (one + two).astype(BF16))
            bit = (cube >> level) & 1
            joined = jnp.where((lane >> 6) == bit, joined, 0.0).astype(BF16)
            order = jnp.where(row == child[12 + level:13 + level, :], 1.0, 0.0).astype(BF16)
            weight = nt(joined, order).astype(BF16)
        out_ref[...] = weight.astype(F32)

    return run(
        body,
        [(ids, SMEM), (near, VMEM), (far, VMEM), (tok, ANY)],
        [((K, K), F32, VMEM)],
        [pltpu.VMEM((16, 16, K), jnp.int32)],
    )


def parts_of(row, rows, weight, tiles, tok):
    def body(weight_ref, tiles_ref, _, keep_ref, send_ref, pool, buf, sem):
        get = pltpu.make_async_copy(tiles_ref.at[:, pl.ds(row, rows), :], pool, sem.at[0])
        get.start()
        w = weight_ref[...].astype(BF16)
        w = jnp.concatenate([w, w], axis=1)
        get.wait()
        flat = pool.reshape(K * rows, TB)
        out = buf.reshape(K * rows, TB)

        def step(n, carry):
            at = n * 2
            x = jnp.concatenate(
                [flat[pl.ds(at, K, stride=rows), :], flat[pl.ds(at + 1, K, stride=rows), :]], axis=1
            )
            y = jnp.dot(w, jnp.concatenate(split2(x), axis=0), preferred_element_type=F32)
            out[pl.ds(at, K, stride=rows), :] = y[:, :TB]
            out[pl.ds(at + 1, K, stride=rows), :] = y[:, TB:]
            return carry

        lax.fori_loop(0, rows // 2, step, 0, unroll=4)
        one = pltpu.make_async_copy(buf.at[pl.ds(0, HALF)], keep_ref, sem.at[1])
        two = pltpu.make_async_copy(buf.at[pl.ds(HALF, HALF)], send_ref, sem.at[2])
        one.start()
        two.start()
        one.wait()
        two.wait()

    return run(
        body,
        [(weight, VMEM), (tiles, ANY), (tok, ANY)],
        [((HALF, rows, TB), F32, ANY)] * 2,
        [pltpu.VMEM((K, rows, TB), F32), pltpu.VMEM((K, rows, TB), F32), DMA((3,))],
    )


def add_cut(terms, cuts, rows, tok):
    def body(*refs):
        total = refs[0][...]
        for term in refs[1:len(terms)]:
            total = total + term[...]
        at = 0
        for cut, ref in zip(cuts, refs[len(terms) + 1:]):
            ref[...] = total[at:at + cut]
            at += cut

    return run(
        body, [(t, VMEM) for t in terms] + [(tok, ANY)], [((cut, rows, TB), F32, VMEM) for cut in cuts], []
    )


def lay(pieces, rows, tok):
    count = sum(p.shape[0] for p in pieces)

    def body(*refs):
        out_ref, sem = refs[-2:]
        copies = []
        at = 0
        for n, piece in enumerate(pieces):
            copies.append(
                pltpu.make_async_copy(refs[n], out_ref.at[pl.ds(at, piece.shape[0])], sem.at[n])
            )
            at += piece.shape[0]
        for copy in copies:
            copy.start()
        for copy in copies:
            copy.wait()

    return run(
        body, [(p, ANY) for p in pieces] + [(tok, ANY)], [((count, rows, TB), pieces[0].dtype, ANY)], [DMA((len(pieces),))]
    )


def prepare(rows, low, high, ids, tok):
    def body(ids_ref, low_ref, high_ref, _, top_ref, rest_ref, pool, sem):
        one = pltpu.make_async_copy(low_ref, pool.at[pl.ds(0, HALF)], sem.at[0])
        two = pltpu.make_async_copy(high_ref, pool.at[pl.ds(HALF, HALF)], sem.at[1])
        one.start()
        two.start()
        mask = ids_ref[4]
        one.wait()
        two.wait()
        for i in range(KR):

            def step(j, c):
                at = pl.ds(pl.multiple_of(j * TB, TB), TB)
                h, lo = split2(pool[jnp.bitwise_xor(i * KC + j, mask)])
                top_ref[i * rows:(i + 1) * rows, at] = h
                rest_ref[i * rows:(i + 1) * rows, at] = lo
                return c

            lax.fori_loop(0, KC, step, 0, unroll=4)

    return run(
        body,
        [(ids, SMEM), (low, ANY), (high, ANY), (tok, ANY)],
        [((KR * rows, KC * TB), BF16, VMEM)] * 2,
        [pltpu.VMEM((K, rows, TB), F32), DMA((2,))],
    )


def arrange(inverse, tok):
    def body(inv_ref, _, top_ref, rest_ref):
        pieces = [inv_ref[:, i * TB + row:i * TB + row + n] for row, n in PARTS for i in range(KR)]
        top_ref[...], rest_ref[...] = split2(jnp.concatenate(pieces, axis=1))

    return run(body, [(inverse, VMEM), (tok, ANY)], [((PW, PW), BF16, VMEM)] * 2, [])


def update(groups, cols, sent, fronts, ids, inverse, pivots, out, tok):
    width = 512
    chunks = [(top + n * rows, rows) for top, rows, count in groups for n in range(count)]
    first = chunks[0][0]
    tall = sum(rows for _, rows in chunks)
    m = KR * tall
    at_pivots = 4 + 2 * len(groups)
    at_fronts = at_pivots + len(pivots)

    def body(ids_ref, inv_ref, low_ref, *refs):
        out_ref, end_ref, left = refs[-3:]
        refs = (ids_ref, inv_ref, low_ref, None) + refs
        end_ref[...] = jnp.zeros_like(end_ref)

        @pl.when(pl.program_id(0) == 0)
        def _():
            at = 0
            for n, (_, rows, count) in enumerate(groups):
                size = KR * rows * count
                own, other = refs[4 + 2 * n], refs[5 + 2 * n]
                h, lo = split2(jnp.where(ids_ref[2] == 0, own[...], other[...]).reshape(size, PW))
                both = jnp.dot(jnp.concatenate([h, lo], axis=0), inv_ref[...], preferred_element_type=F32)
                total = both[:size] + both[size:] + jnp.dot(h, low_ref[...], preferred_element_type=F32)
                left[at:at + size, :], left[m + at:m + at + size, :] = split2(total)
                at += size

        at, total = 0, 0.0
        for n, (_, size) in enumerate(PARTS):
            h = left[:, at:at + KR * size]
            both = jnp.dot(h, refs[at_pivots + 2 * n][...], preferred_element_type=F32)
            total += both[:m] + both[m:] + jnp.dot(h[:m], refs[at_pivots + 2 * n + 1][...], preferred_element_type=F32)
            at += KR * size
        at = 0
        for n, (row, rows) in enumerate(chunks):
            one = total[at:at + KR * rows].reshape(KR, rows, width)
            out_ref[:, row - first:row - first + rows, :] = refs[at_fronts + n][...] - one
            at += KR * rows

    square = pl.BlockSpec((PW, PW), lambda n: (0, 0))
    ins = [(ids, SMEM), (inverse[0], square), (inverse[1], square)]
    for (_, rows, count), own, other in zip(groups, cols, sent):
        pivot = pl.BlockSpec((count, KR, rows, PW), lambda n: (0, 0, 0, 0))
        ins += [(own, pivot), (other, pivot)]
    ins += [(p, pl.BlockSpec((p.shape[0], width), lambda n: (0, n))) for p in pivots]
    ins += [(f, pl.BlockSpec((KR, f.shape[1], width), lambda n: (0, 0, n))) for f in fronts]
    ins.append((tok, ANY))
    more = {}
    if out is not None:
        ins.append((out, ANY))
        more["input_output_aliases"] = {len(ins) - 1: 0}
    return run(
        body,
        ins,
        [
            ((KR, TB, KC * TB), F32, pl.BlockSpec((KR, tall, width), lambda n: (0, first // tall, n))),
            ((8, TB), F32, pl.BlockSpec((8, TB), lambda n: (0, 0))),
        ],
        [pltpu.VMEM((2 * m, PW), BF16)],
        limit=24,
        grid=(KC * TB // width,),
        **more,
    )


class Plan:
    def __init__(self):
        self.steps, self.kernels = [], []

    def kernel(self, name, need, give, cost, call):
        self.kernels.append(name)
        self.steps.append((name, "kernel", need, give, cost, call))

    def permute(self, name, need, give, links, cost, call):
        self.steps.append((name, "permute", [need], [give], (links, cost), call))

    def emit(self):
        steps = {s[0]: s for s in self.steps}
        for number in ORDER:
            step = steps[self.kernels[number]]
            yield number, step
            for s in self.steps:
                if s[1] == "permute" and s[2][0] in step[3]:
                    yield None, s


def text(*parts):
    return "".join(str(p) for p in parts)


def flip(axis, bits):
    return lambda v: lax.ppermute(v, axis, [(i, i ^ bits) for i in range(lax.axis_size(axis))])


def make_plan(tiles, split, first, second, ids, pivot_inverse):
    level_links = (("core",), ("xa",), ("xa", "xb"), ("y",))
    link_time = (3.5, 22.8, 22.8, 22.8)
    plan = Plan()
    kernel, permute = plan.kernel, plan.permute

    def level_steps(group, index):
        top, rows, count = group
        row = top + index * rows
        n, g = text("c", row), text("g", top)
        share = rows / 32
        kernel(text(n, "k0"), [], [text(n, "s0"), text(n, "h0")], 0.6 + 0.4 * share, lambda v, tok: first_split(row, rows, tiles, split, tok))
        for level in range(LEVELS):
            permute(text(n, "p", level), text(n, "s", level), text(n, "r", level), level_links[level], link_time[level] * share, flip("cube", 1 << level))
            need = [text(n, "r", level), text(n, "h", level)]
            if level < LEVELS - 1:
                kernel(
                    text(n, "k", level + 1),
                    need,
                    [text(n, "s", level + 1), text(n, "h", level + 1)],
                    0.8 + 0.9 * share,
                    lambda v, tok, level=level: next_level(
                        level, rows, v[text(n, "h", level)], v[text(n, "r", level)], split, first, second, tok
                    ),
                )
            else:
                kernel(
                    text(n, "k4"),
                    need + ([text(g, "cols", index - 1)] if index else []),
                    [text(g, "cols", index), text(n, "front")],
                    0.8 + 0.9 * share,
                    lambda v, tok: last_level(
                        index, count, rows, v[text(n, "h3")], v[text(n, "r3")], first, second, v.get(text(g, "cols", index - 1)), tok
                    ),
                )
        if index == count - 1:
            permute(
                text(g, "pc"), text(g, "cols", index), text(g, "sent"), ("y",), 5.7 * share * count,
                lambda v: lax.ppermute(v, "col", [(0, 1)]),
            )

    def part_steps(index, row, rows):
        n = text("q", index)
        m = rows / 128

        def add(name, terms, cuts, cost):
            kernel(
                text(n, name), [text(n, t) for t in terms], [text(n, name, i) for i in range(len(cuts))], cost,
                lambda v, tok: add_cut([v[text(n, t)] for t in terms], cuts, rows, tok),
            )

        def move(name, what, axis, bits, links, cost):
            permute(text(n, name), text(n, what), text(n, name), links, cost, flip(axis, bits))

        def join(name, pieces, cost):
            kernel(text(n, name), [text(n, p) for p in pieces], [text(n, name)], cost, lambda v, tok: lay([v[text(n, p)] for p in pieces], rows, tok))

        kernel(text(n, "t"), ["weight"], [text(n, "keep"), text(n, "send")], 2 + 6 * m, lambda v, tok: parts_of(row, rows, v["weight"], tiles, tok))
        move("core", "send", "cube", 1, ("core",), 7 * m)
        add("a", ["keep", "core"], (64,), 0.5 + 2 * m)
        permute(text(n, "zs"), text(n, "a0"), text(n, "zs"), ("gather",), 16 + 30 * m, lambda v: lax.psum_scatter(v, "row", tiled=True))
        add("b", ["zs"], (8, 8), 0.5 + m)
        move("y", "b1", "cube", 8, ("y",), 11.4 * m)
        add("c", ["b0", "y"], (8,), 0.5)
        move("xa", "c0", "cube", 2, ("xa",), 11.4 * m)
        add("d", ["c0", "xa"], (8,), 0.5)
        move("xb", "d0", "cube", 6, ("xb",), 11.4 * m)
        add("e", ["d0", "xb"], (8,), 0.5)
        move("gy", "e0", "cube", 8, ("y",), 11.4 * m)
        join("h", ["e0", "gy"], 1)
        permute(text(n, "gz"), text(n, "h"), text(n, "gz"), ("gather",), 16 + 30 * m, lambda v: lax.all_gather(v, "row", tiled=True))
        join("low", ["gz"], 1 + 2 * m)
        move("high", "low", "cube", 1, ("core",), 7 * m)
        kernel(text(n, "m"), [text(n, "low"), text(n, "high")], [text(n, "m0"), text(n, "m1")], 4, lambda v, tok: prepare(rows, v[text(n, "low")], v[text(n, "high")], ids, tok))

    level_steps(GROUPS[0], 0)
    kernel("l0", [], ["ls0"], 0.6, lambda v, tok: own_lists(split, first, second, tok))
    for n, bits in enumerate((2, 4, 8, 1)):
        permute(text("lp", n), text("ls", n), text("lr", n), level_links[(1, 2, 3, 0)[n]], 0.2, flip("cube", bits))
        if n < 3:
            kernel(text("l", n + 1), [text("ls", n), text("lr", n)], [text("ls", n + 1)], 0.5, lambda v, tok, n=n: lay([v[text("ls", n)], v[text("lr", n)]], 16, tok))
    kernel("weight", ["ls3", "lr3"], ["weight"], 1.5, lambda v, tok: weights(ids, v["ls3"], v["lr3"], tok))
    for group in GROUPS:
        for index in range(group[2]):
            if group is not GROUPS[0] or index:
                level_steps(group, index)
    for index, part in enumerate(PARTS):
        part_steps(index, *part)
    kernel("inv", [], ["inv0", "inv1"], 2, lambda v, tok: arrange(pivot_inverse, tok))
    pivots = [text("q", i, "m", j) for i in range(len(PARTS)) for j in range(2)]
    start = 0
    for at, number in enumerate(CALLS):
        groups = GROUPS[start:start + number]
        start += number
        cols = [text("g", top, "cols", count - 1) for top, rows, count in groups]
        sent = [text("g", top, "sent") for top, rows, count in groups]
        fronts = [text("c", top + n * rows, "front") for top, rows, count in groups for n in range(count)]
        kernel(
            text("u", at), fronts + cols + sent + pivots + ["inv0", "inv1"] + ([text("out", at - 1)] if at else []), [text("out", at)], 8,
            lambda v, tok, at=at, groups=groups, names=(cols, sent, fronts): update(
                groups, *[[v[n] for n in x] for x in names], ids, (v["inv0"], v["inv1"]), [v[p] for p in pivots], v.get(text("out", at - 1)), tok
            ),
        )

    return plan


def body(update_tiles, split_order, first_source, second_source, pivot_inverse):
    tiles = pltpu.with_memory_space_constraint(update_tiles.reshape(K, TB, TB), pltpu.HBM)
    split, first, second = (x.reshape(LEVELS, K) for x in (split_order, first_source, second_source))
    cube, row_at, col = lax.axis_index("cube"), lax.axis_index("row"), lax.axis_index("col")
    mask = (cube & 1) * 64 + row_at * 16 + (cube >> 3) * 8
    ids = jnp.stack([cube, row_at, col, mask, mask - row_at * 16]).astype(jnp.int32)
    plan = make_plan(tiles, split, first, second, ids, pivot_inverse)
    values = {}
    tok = ids
    for number, (name, kind, need, give, _, call) in plan.emit():
        if number is not None:
            FLOPS[0] = int(WORK.get(number, 0) * 2.2e10)
            with jax.named_scope(name):
                results = call(values, tok)
            tok = results[1] if give[0].startswith("out") else results[0]
            values.update(zip(give, results))
        else:
            with jax.named_scope(name):
                values[give[0]] = call(values[need[0]])
    return values[text("out", len(CALLS) - 1)].reshape(1, 1, 1, KR * TB, KC * TB)


def solution(mesh):
    return jax.shard_map(
        body,
        mesh=mesh,
        in_specs=(
            P("cube", "row", "col", None, None, None),
            P("cube", "row", "col", None, None),
            P("cube", "row", "col", None, None),
            P("cube", "row", "col", None, None),
            P(),
        ),
        out_specs=P("cube", "row", "col", None, None),
        check_vma=False,
    )
```
